512 devices in a mesh: inst: 32 (over y_hi, z), tp: 16 (over x, y_lo, core).
Axes of the slice: x: 4, y: 4 (y_hi: 2, y_lo: 2; y = y_hi * 2 + y_lo), z: 16, core: 2. Of those that a mesh axis runs over, the one named last changes fastest.
Arguments:
- queries: bfloat16 [2, 3072, 64, 128], P(None, 'inst', 'tp'), may hold values from -8 to 50
- row_prompt: int32 [3072], P('inst'), may hold values from 0 to 47, as said below
- owner_slot: int32 [48], replicated, may hold values from 0 to 63, as said below
- suffix_len: int32 [3072], P('inst'), may hold values from 1 to 8
- prefix_keys: bfloat16 [64, 4096, 16, 128], P('inst', None, 'tp'), may hold values from -4.5 to 50, as said below
- prefix_values: bfloat16 [64, 4096, 16, 128], P('inst', None, 'tp'), may hold values from -8 to 8, as said below
- suffix_keys: bfloat16 [3072, 8, 16, 128], P('inst', None, 'tp'), may hold values from -12 to 12, as said below
- suffix_values: bfloat16 [3072, 8, 16, 128], P('inst', None, 'tp'), may hold values from -8 to 8, as said below
- new_keys: bfloat16 [2, 3072, 16, 128], P(None, 'inst', 'tp'), may hold values from -12 to 12, as said below
- new_values: bfloat16 [2, 3072, 16, 128], P(None, 'inst', 'tp'), may hold values from -8 to 8, as said below
- out_weight: bfloat16 [8192, 2560], P('tp'), may hold values from -0.0625 to 0.0625
Outputs:
- projected: bfloat16 [3072, 2, 2560], P(('inst', 'tp'))
The draws below stay inside these ranges and needn't reach their ends.
Inputs may be any that keep to these rules, and one draw needn't show every extreme that they name: `row_prompt`: samples come in consecutive blocks of 64, one prompt each, every prompt in exactly one block. `owner_slot`: different prompts have different slots. `prefix_keys`: copies of one key-value head are equal. `prefix_values`: copies of one key-value head are equal. `suffix_keys`: copies of one key-value head are equal. `suffix_values`: copies of one key-value head are equal. `new_keys`: copies of one key-value head are equal. `new_values`: copies of one key-value head are equal.
All inputs are finite; a program needn't handle non-finite values.
Results may differ from the reference program's by a relative error of at most 0.0052.
Values may be sent and summed in bfloat16 or wider, within the bound.
A program may use at most 128 MiB of HBM per device.

```python
import math
import jax
import jax.numpy as jnp
from jax import lax

D = 2560
QH = 64
KVH = 8
HD = 128
GROUP = 64
STEPS = 2
PREFIX = 4096
SUFFIX = 8
KVC = 16
TOTAL_ROWS = 3072
PROMPTS = 48
OWN = 2
SLOTS = 64


def copied_heads(values):
    return jnp.repeat(values, KVC // KVH, axis=2)


def copied_normal(key, lead_shape, scale, bound):
    shape = lead_shape + (KVH, HD)
    values = jnp.clip(scale * jax.random.normal(key, shape, jnp.float32), -bound, bound)
    return copied_heads(values)


def prompt_order(key):
    return jax.random.permutation(jax.random.fold_in(key, 7), PROMPTS).astype(jnp.int32)


def placed_value(table, index, value):
    found = jnp.argmax(table == value)
    moved = table[index]
    table = table.at[found].set(moved)
    return table.at[index].set(value)


def draw_queries(key, part):
    key = jax.random.fold_in(key, 11)
    shape = (STEPS, TOTAL_ROWS, QH, HD)
    base_key = jax.random.fold_in(key, 0)
    return jnp.clip(2.0 * jax.random.normal(base_key, shape, jnp.float32), -8.0, 8.0).astype(jnp.bfloat16)


def draw_prefix_keys(key, part):
    key = jax.random.fold_in(key, 12)
    shape = (SLOTS, PREFIX, KVH, HD)
    base_key = jax.random.fold_in(key, 0)
    return copied_heads(jnp.clip(jax.random.normal(base_key, shape, jnp.float32), -4.5, 4.5)).astype(jnp.bfloat16)


def draw_prefix_values(key, part):
    key = jax.random.fold_in(key, 16)
    return copied_normal(key, (SLOTS, PREFIX), 2.0, 8.0).astype(jnp.bfloat16)


def draw_suffix_keys(key, part):
    key = jax.random.fold_in(key, 17)
    return copied_normal(key, (TOTAL_ROWS, SUFFIX), 3.0, 12.0).astype(jnp.bfloat16)


def draw_suffix_values(key, part):
    key = jax.random.fold_in(key, 18)
    return copied_normal(key, (TOTAL_ROWS, SUFFIX), 2.0, 8.0).astype(jnp.bfloat16)


def draw_new_keys(key, part):
    key = jax.random.fold_in(key, 19)
    return copied_normal(key, (STEPS, TOTAL_ROWS), 3.0, 12.0).astype(jnp.bfloat16)


def draw_new_values(key, part):
    key = jax.random.fold_in(key, 20)
    return copied_normal(key, (STEPS, TOTAL_ROWS), 2.0, 8.0).astype(jnp.bfloat16)


def draw_suffix_len(key, part):
    key = jax.random.fold_in(key, 13)
    length_key, place_key = jax.random.split(key)
    lengths = jax.random.randint(length_key, (TOTAL_ROWS,), 1, SUFFIX + 1)
    full_spot = jax.random.randint(place_key, (TOTAL_ROWS // 16, 1), 0, 16)
    full = (jnp.arange(16)[None, :] == full_spot).reshape(TOTAL_ROWS)
    return jnp.where(full, SUFFIX, lengths).astype(jnp.int32)


def draw_row_prompt(key, part):
    order = prompt_order(key)
    return order[jnp.arange(TOTAL_ROWS) // GROUP]


def draw_owner_slot(key, part):
    order = prompt_order(key)
    key = jax.random.fold_in(key, 15)
    shuffled = jax.random.permutation(key, SLOTS).astype(jnp.int32)
    first_prompt = order[0]
    far_slot = SLOTS // OWN // 2 * OWN
    shuffled = placed_value(shuffled, first_prompt, far_slot)
    shuffled = placed_value(shuffled, (first_prompt + 1) % PROMPTS, SLOTS - 1)
    shuffled = placed_value(shuffled, (first_prompt + 2) % PROMPTS, 0)
    return shuffled[:PROMPTS].astype(jnp.int32)


def level_of(key, extent, pieces, least, largest):
    factor_of, own = 1.0, jax.random.fold_in(key, 6)
    for position, blocks in pieces:
        heights = jnp.exp(jax.random.uniform(jax.random.fold_in(own, position), (blocks,), jnp.float32, least / len(pieces), largest / len(pieces)))
        factor_of = factor_of * jnp.repeat(heights, extent[position] // blocks).reshape([-1 if axis == position else 1 for axis in range(len(extent))])
    return factor_of


def centred(key, extent, scale, most, cuts=(), dtype=jnp.bfloat16):
    array = scale * jax.random.normal(key, extent, jnp.float32)
    if cuts:
        array = array * level_of(key, extent, cuts, -0.22, 0.18)
    return jnp.clip(array, -most, most).astype(dtype)


def setup_inputs(seed: int = 0) -> dict:
    key_list = jax.random.split(jax.random.key(seed), 12)
    return {
        "queries": draw_queries(jax.random.fold_in(key_list[11], 71), 0),
        "row_prompt": draw_row_prompt(jax.random.fold_in(key_list[11], 71), 0),
        "owner_slot": draw_owner_slot(jax.random.fold_in(key_list[11], 71), 0),
        "suffix_len": draw_suffix_len(jax.random.fold_in(key_list[11], 71), 0),
        "prefix_keys": draw_prefix_keys(jax.random.fold_in(key_list[11], 71), 0),
        "prefix_values": draw_prefix_values(jax.random.fold_in(key_list[11], 71), 0),
        "suffix_keys": draw_suffix_keys(jax.random.fold_in(key_list[11], 71), 0),
        "suffix_values": draw_suffix_values(jax.random.fold_in(key_list[11], 71), 0),
        "new_keys": draw_new_keys(jax.random.fold_in(key_list[11], 71), 0),
        "new_values": draw_new_values(jax.random.fold_in(key_list[11], 71), 0),
        "out_weight": centred(key_list[10], (QH * HD, D), (QH * HD) ** -0.5, 0.0625, ((0, 16),)),
    }


def rounded(values):
    return lax.optimization_barrier(values.astype(jnp.bfloat16)).astype(jnp.float32)

def prefix_part(query_block, key_block, value_block):
    step_count, row_count, head_count, head_width = query_block.shape
    copy_count = key_block.shape[1]
    grouped = query_block.reshape(step_count, row_count, copy_count, head_count // copy_count, head_width).astype(jnp.float32)
    scores = jnp.einsum('tbcrd,pcd->tbcrp', grouped, key_block.astype(jnp.float32)) / math.sqrt(head_width)
    highest = lax.optimization_barrier(jnp.max(scores, axis=-1))
    weights_raw = jnp.exp(scores - highest[..., None])
    weight_sum = lax.optimization_barrier(jnp.sum(weights_raw, axis=-1))
    summed = jnp.einsum('tbcrp,pcd->tbcrd', rounded(weights_raw), value_block.astype(jnp.float32))
    output = (summed / weight_sum[..., None]).astype(jnp.bfloat16).reshape(step_count, row_count, head_count, head_width)
    log_total = (highest + jnp.log(weight_sum)).reshape(step_count, row_count, head_count)
    return (output, log_total)

def combine(queries, prefix_out, prefix_total, suffix_len, suffix_keys, suffix_values, new_keys, new_values):
    step_count, row_count, head_count, head_width = queries.shape
    copy_count = suffix_keys.shape[2]
    cache_len = suffix_keys.shape[1]
    all_keys = jnp.concatenate([suffix_keys, jnp.swapaxes(new_keys, 0, 1)], axis=1).astype(jnp.float32)
    all_values = jnp.concatenate([suffix_values, jnp.swapaxes(new_values, 0, 1)], axis=1).astype(jnp.float32)
    grouped = queries.reshape(step_count, row_count, copy_count, head_count // copy_count, head_width).astype(jnp.float32)
    scores = jnp.einsum('trcxd,rjcd->trcxj', grouped, all_keys) / math.sqrt(head_width)
    key_slots = jnp.arange(cache_len + step_count)
    step_ids = jnp.arange(step_count)
    live = jnp.where(key_slots[None, None, :] < cache_len, key_slots[None, None, :] < suffix_len[None, :, None], key_slots[None, None, :] - cache_len <= step_ids[:, None, None])
    masked = jnp.where(live[:, :, None, None, :], scores, -jnp.inf)
    carried = prefix_total.reshape(step_count, row_count, copy_count, head_count // copy_count)
    highest = jnp.maximum(carried, lax.optimization_barrier(jnp.max(masked, axis=-1)))
    weights_raw = jnp.exp(masked - highest[..., None])
    share = jnp.exp(carried - highest)
    denominator = share + lax.optimization_barrier(jnp.sum(weights_raw, axis=-1))
    mixed = jnp.einsum('trcxj,rjcd->trcxd', rounded(weights_raw), all_values)
    earlier = prefix_out.reshape(step_count, row_count, copy_count, head_count // copy_count, head_width).astype(jnp.float32)
    numerator = share[..., None] * earlier + mixed
    attended = (numerator / denominator[..., None]).astype(jnp.bfloat16)
    return attended.reshape(step_count, row_count, head_count * head_width)

def reference(queries, row_prompt, owner_slot, suffix_len, prefix_keys, prefix_values, suffix_keys, suffix_values, new_keys, new_values, out_weight):
    blocks = jnp.transpose(queries.reshape(STEPS, PROMPTS, GROUP, QH, HD), (1, 0, 2, 3, 4))
    block_slot = owner_slot[row_prompt[::GROUP]]

    def one_prompt(item):
        query_block, slot_index = item
        return prefix_part(query_block, prefix_keys[slot_index], prefix_values[slot_index])
    prefix_out, prefix_total = lax.map(one_prompt, (blocks, block_slot))
    prefix_out = jnp.transpose(prefix_out, (1, 0, 2, 3, 4)).reshape(STEPS, TOTAL_ROWS, QH, HD)
    prefix_total = jnp.transpose(prefix_total, (1, 0, 2, 3)).reshape(STEPS, TOTAL_ROWS, QH)
    attended = combine(queries, prefix_out, prefix_total, suffix_len, suffix_keys, suffix_values, new_keys, new_values)
    flat_rows = attended.reshape(STEPS * TOTAL_ROWS, QH * HD)
    projected = jnp.dot(flat_rows, out_weight, preferred_element_type=jnp.float32).reshape(STEPS, TOTAL_ROWS, D)
    return jnp.transpose(projected, (1, 0, 2)).astype(jnp.bfloat16)
```

```python
import math

import jax
import jax.numpy as jnp
from jax import lax
from jax.experimental import pallas as pl
from jax.experimental.pallas import tpu as pltpu
from jax.sharding import PartitionSpec as P

F32 = jnp.float32
BF16 = jnp.bfloat16
I32 = jnp.int32

NI = 32
NZ = 16
HALVES = 3
BLOCKS = 48
SLOTS = 64
OWN = 2
HD = 128
KEYS = 4096
D = 2560
CH = 512
NCH = D // CH
KC = 512
SCALE = 1.0 / math.sqrt(HD)
C2 = SCALE * math.log2(math.e)
NEG = -1e30


def dot_t(a, b):
    return lax.dot_general(a, b, (((1,), (1,)), ((), ())), preferred_element_type=F32)


def dot(a, b):
    return lax.dot_general(a, b, (((1,), (0,)), ((), ())), preferred_element_type=F32)


def iota(shape, dim):
    return lax.broadcasted_iota(I32, shape, dim)


def kernel(
    row_prompt,
    owner_slot,
    lens,
    q_hbm,
    k_hbm,
    v_hbm,
    sk_hbm,
    sv_hbm,
    nk_hbm,
    nv_hbm,
    w_hbm,
    out,
    q,
    kk,
    va,
    ck,
    cv,
    w,
    tab,
    inv_v,
    inv_s,
    mid,
    snd,
    qin,
    scores,
    obuf,
    tbuf,
    mid2,
    tmid,
    snd2,
    tsnd,
    pin,
    tin,
    own_acc,
    own_m,
    own_l,
    att,
    lhs,
    mine,
    cs,
    cr,
    xs,
    xr,
    sums,
    ld,
    ss,
    rs,
    css,
    crs,
    xss,
    xrs,
):
    inst = lax.axis_index("inst")
    tp = lax.axis_index("tp")
    yy = lax.div(inst, NZ)
    zz = lax.rem(inst, NZ)
    core = lax.rem(tp, 2)
    chip = lax.div(tp, 2)
    partner = tp + 1 - 2 * core

    def remote(src, dst, s, r, **where):
        return pltpu.make_async_remote_copy(
            src_ref=src, dst_ref=dst, send_sem=s, recv_sem=r,
            device_id=where, device_id_type=pl.DeviceIdType.MESH,
        )

    def local(src, dst, s):
        return pltpu.make_async_copy(src, dst, s)

    def chip_at(step):
        return lax.rem(chip + step, 8) * 2 + core

    load_q = local(q_hbm, q, ld.at[0])
    load_q.start()
    loads_own = []
    for u in range(HALVES):
        for src, dst, sem in ((sk_hbm, ck, 3), (sv_hbm, cv, 4)):
            loads_own.append(
                local(src.at[pl.ds(256 * u, 256)], dst.at[u, pl.ds(0, 256)], ld.at[sem + 4 * u])
            )
        for src, dst, sem in ((nk_hbm, ck, 5), (nv_hbm, cv, 6)):
            loads_own.append(
                local(
                    src.at[:, pl.ds(32 * u, 32)],
                    dst.at[u, pl.ds(256, 64)].reshape(2, 32, HD),
                    ld.at[sem + 4 * u],
                )
            )
    for c in loads_own:
        c.start()
    load_k = local(k_hbm, kk, ld.at[1])
    load_k.start()
    load_v = local(v_hbm, va.at[:, :, pl.ds(0, HD)], ld.at[2])
    load_v.start()
    load_w = local(w_hbm, w, ld.at[15])
    load_w.start()

    barrier = pltpu.get_barrier_semaphore()

    def greet(n, _):
        pl.semaphore_signal(
            barrier, inc=1, device_id={"inst": lax.rem(inst + n, NI)},
            device_id_type=pl.DeviceIdType.MESH,
        )
        return 0

    lax.fori_loop(1, NI, greet, 0)
    pl.semaphore_signal(
        barrier, inc=1, device_id={"tp": partner}, device_id_type=pl.DeviceIdType.MESH
    )

    def greet_chip(n, _):
        pl.semaphore_signal(
            barrier, inc=1, device_id={"tp": chip_at(n)}, device_id_type=pl.DeviceIdType.MESH
        )
        return 0

    lax.fori_loop(1, 8, greet_chip, 0)

    rows4 = iota((4, HD), 0)
    head = jnp.full((4, HD), 255, I32)
    for u in range(HALVES):
        head = jnp.where(rows4 == u, owner_slot[row_prompt[32 * u]], head)
    tab[inst] = head
    ones = jnp.ones((256, HD), BF16)

    def set_ones(n, _):
        va[lax.div(n, 16), pl.ds(pl.multiple_of(lax.rem(n, 16) * 256, 256), 256), pl.ds(HD, HD)] = ones
        return 0

    lax.fori_loop(0, 32, set_ones, 0)
    for u in range(HALVES):
        ck[u, pl.ds(320, 64)] = jnp.zeros((64, HD), BF16)
        cv[u, pl.ds(320, 64)] = jnp.zeros((64, HD), BF16)

    pl.semaphore_wait(barrier, NI - 1 + 1 + 7)

    def send_head(n, _):
        remote(
            tab.at[inst], tab.at[inst], ss.at[0], rs.at[0], inst=lax.rem(inst + n, NI)
        ).start()
        return 0

    lax.fori_loop(1, NI, send_head, 0)

    load_q.wait()

    def piece_of(u, m):
        t = lax.div(m, 8)
        at = pl.multiple_of(128 * u + 16 * lax.rem(m, 8), 16)
        return q.at[t, pl.ds(at, 16)]

    def block_at(u):
        return lax.div(HALVES * inst + u, 2)

    for u in range(HALVES):
        side = lax.rem(zz + u, 2)

        @pl.when(side == yy)
        def _():
            local(piece_of(u, zz), mid.at[block_at(u)], rs.at[1]).start()

        @pl.when(side != yy)
        def _():
            remote(piece_of(u, zz), mid.at[block_at(u)], ss.at[1], rs.at[1], inst=side * NZ + zz).start()

    def send_piece(n, _):
        m = lax.rem(zz + n, NZ)
        for u in range(HALVES):
            side = lax.rem(zz + u, 2)
            remote(piece_of(u, m), mid.at[block_at(u)], ss.at[1], rs.at[1], inst=side * NZ + m).start()
        return 0

    lax.fori_loop(1, NZ, send_piece, 0)

    for c in loads_own:
        c.wait()
    lens_b = jnp.broadcast_to(lens[...].astype(F32), (8, 96)).astype(BF16)
    for u in range(HALVES):
        at96 = iota((96, 384), 0)
        lane96 = iota((96, 384), 1)
        spread = jnp.where(at96 == 32 * u + lax.div(lane96, 8), 1.0, 0.0).astype(BF16)
        len_row = dot(lens_b, spread)[0:1]
        row = iota((256, 384), 0)
        lane = iota((256, 384), 1)
        sample = lax.div(lax.rem(row, 128), 4)
        step = lax.div(row, 128)
        cached = (lane < 256) & (lax.div(lane, 8) == sample) & (
            lax.rem(lane, 8).astype(F32) < jnp.broadcast_to(len_row, (256, 384))
        )
        new_at = lane - 256
        new = (lane >= 256) & (lane < 320) & (lax.rem(new_at, 32) == sample) & (
            lax.div(new_at, 32) <= step
        )
        qu = jnp.concatenate([q[0, pl.ds(128 * u, 128)], q[1, pl.ds(128 * u, 128)]], axis=0)
        s = jnp.where(cached | new, dot_t(qu, ck[u]), NEG)
        top = jnp.max(s, axis=1, keepdims=True)
        p = jnp.exp2(s * C2 - top * C2)
        own_m[u] = jnp.broadcast_to(top * SCALE, (256, HD))
        own_l[u] = jnp.broadcast_to(jnp.sum(p, axis=1, keepdims=True), (256, HD))
        own_acc[u] = dot(p.astype(BF16), cv[u])

    heads_all = tab.at[pl.ds(0, NI - 1)]
    local(heads_all, heads_all, rs.at[0]).wait()
    t4 = tab[...]
    g = HALVES * iota((NI, 4, HD), 0) + iota((NI, 4, HD), 1)
    lane3 = iota((NI, 4, HD), 2)
    first = (iota((NI, 4, HD), 1) < HALVES) & (lax.rem(g, 2) == 0)
    block = lax.div(g, 2)
    of_slot = jnp.sum(jnp.where(first & (t4 == lane3), block, 0), axis=0)
    of_block = jnp.sum(jnp.where(first & (block == lane3), t4, 0), axis=0)
    inv_v[pl.ds(0, 4)] = of_slot
    inv_v[pl.ds(4, 4)] = of_block
    to_smem = local(inv_v, inv_s, ld.at[16])
    to_smem.start()
    to_smem.wait()

    def slot_block(s):
        return jnp.clip(inv_s[0, s] + inv_s[1, s] + inv_s[2, s], 0, BLOCKS - 1)

    def block_slot(n):
        return jnp.clip(inv_s[4, n] + inv_s[5, n] + inv_s[6, n], 0, SLOTS - 1)

    local(mid, mid, rs.at[1]).wait()
    for e in range(OWN):
        def select(d, _):
            snd[e, d] = mid[slot_block(OWN * d + e)]
            return 0

        lax.fori_loop(0, NI, select, 0)
        local(snd.at[e, inst], qin.at[e, inst], rs.at[2 + e]).start()

        def send(n, _):
            d = lax.rem(inst + n, NI)
            remote(snd.at[e, d], qin.at[e, inst], ss.at[2 + e], rs.at[2 + e], inst=d).start()
            return 0

        lax.fori_loop(1, NI, send, 0)

    load_k.wait()
    load_v.wait()
    eye = iota((HD, HD), 0) == iota((HD, HD), 1)
    run_of = lax.div(iota((1, HD), 1), 16)
    for e in range(OWN):
        local(qin.at[e], qin.at[e], rs.at[2 + e]).wait()
        for y in range(2):
            qv = qin[e, pl.ds(16 * y, 16)].reshape(256, HD)
            top = None
            for c in range(KEYS // KC):
                s = dot_t(qv, kk[e, pl.ds(KC * c, KC)])
                scores[:, pl.ds(KC * c, KC)] = s
                for j in range(KC // HD):
                    part = s[:, HD * j : HD * (j + 1)]
                    top = part if top is None else jnp.maximum(top, part)
            top = jnp.max(top, axis=1, keepdims=True)
            shift = top * C2
            acc = jnp.zeros((256, 2 * HD), F32)
            for c in range(KEYS // KC):
                p = jnp.exp2(scores[:, pl.ds(KC * c, KC)] * C2 - shift)
                acc += dot(p.astype(BF16), va[e, pl.ds(KC * c, KC)])
            weight = acc[:, HD:]
            obuf[e, pl.ds(16 * y, 16)] = (acc[:, :HD] / weight).astype(BF16).reshape(16, 16, HD)
            total = top * SCALE + jnp.log(weight)
            for t in range(2):
                vec = jnp.sum(
                    jnp.where(eye, total[HD * t : HD * (t + 1)], 0.0), axis=0, keepdims=True
                )
                for m in range(8):
                    tbuf[e, 16 * y + 8 * t + m] = jnp.where(run_of == m, vec, 0.0)
        at = OWN * inst + e
        local(obuf.at[e, inst], mid2.at[at], rs.at[4]).start()
        local(tbuf.at[e, inst], tmid.at[at], rs.at[5]).start()

        def back(n, _):
            j = lax.rem(inst + n, NI)
            remote(obuf.at[e, j], mid2.at[at], ss.at[4], rs.at[4], inst=j).start()
            remote(tbuf.at[e, j], tmid.at[at], ss.at[5], rs.at[5], inst=j).start()
            return 0

        lax.fori_loop(1, NI, back, 0)

    local(mid2, mid2, rs.at[4]).wait()
    local(tmid, tmid, rs.at[5]).wait()

    def select2(n, _):
        at = block_slot(n)
        snd2[n] = mid2[at]
        tsnd[n] = tmid[at]
        return 0

    lax.fori_loop(0, BLOCKS, select2, 0)
    first_n = lax.div(HALVES * inst + 1, 2)

    def home(k, _):
        n = lax.rem(first_n + k, BLOCKS)
        gg = 2 * n + yy
        d = lax.div(gg, HALVES)
        u = lax.rem(gg, HALVES)

        @pl.when(d == inst)
        def _():
            local(snd2.at[n], pin.at[u, zz], rs.at[6]).start()
            local(tsnd.at[n], tin.at[u, zz], rs.at[7]).start()

        @pl.when(d != inst)
        def _():
            remote(snd2.at[n], pin.at[u, zz], ss.at[6], rs.at[6], inst=d).start()
            remote(tsnd.at[n], tin.at[u, zz], ss.at[7], rs.at[7], inst=d).start()

        return 0

    lax.fori_loop(0, BLOCKS, home, 0)
    load_w.wait()
    local(pin, pin, rs.at[6]).wait()
    local(tin, tin, rs.at[7]).wait()

    for u in range(HALVES):
        for t in range(2):
            vec = tin[u, 8 * t]
            for m in range(1, 8):
                vec = vec + tin[u, 8 * t + m]
            total = jnp.sum(
                jnp.where(eye, jnp.broadcast_to(vec, (HD, HD)), 0.0), axis=1, keepdims=True
            )
            rows = pl.ds(HD * t, HD)
            own_top = own_m[u, rows]
            top = jnp.maximum(total, own_top)
            carried = jnp.exp(total - top)
            own = jnp.exp(own_top - top)
            below = carried + own * own_l[u, rows]
            before = pin[u, pl.ds(8 * t, 8)].reshape(HD, HD).astype(F32)
            att[t, pl.ds(HD * u, HD)] = (carried * before + own * own_acc[u, rows]) / below
    for t in range(2):
        att[t, pl.ds(384, 16)] = jnp.zeros((16, HD), F32)

    for c in range(2):
        for a in range(8):
            k = 2 * a + c
            for h in range(4):
                pair = [att[t, pl.ds(24 * k + h, 8, stride=4)] for t in range(2)]
                lhs[pl.ds(128 * c + 16 * a, 16), pl.ds(HD * h, HD)] = jnp.concatenate(
                    pair, axis=0
                ).astype(BF16)

    kept = pl.ds(pl.multiple_of(core * 128, 128), 128)
    given = pl.ds(pl.multiple_of((1 - core) * 128, 128), 128)
    for c in range(NCH):
        cs[c] = dot(lhs[given], w[:, pl.ds(CH * c, CH)]).astype(BF16)
        remote(cs.at[c], cr.at[c], css.at[c], crs.at[c], tp=partner).start()
    for c in range(NCH):
        mine[c] = dot(lhs[kept], w[:, pl.ds(CH * c, CH)])
    for c in range(NCH):
        remote(cs.at[c], cr.at[c], css.at[c], crs.at[c], tp=partner).wait_recv()
        both = mine[c] + cr[c].astype(F32)
        sums[c] = both.reshape(8, 16, CH)
        xs[c] = both.astype(BF16).reshape(8, 16, CH)

        def spread_out(n, _):
            remote(
                xs.at[c, lax.rem(chip + n, 8)], xr.at[c, n - 1], xss.at[c], xrs.at[c], tp=chip_at(n)
            ).start()
            return 0

        lax.fori_loop(1, 8, spread_out, 0)
    for c in range(NCH):
        local(xr.at[c], xr.at[c], xrs.at[c]).wait()
        total = sums[c, chip]
        for n in range(7):
            total = total + xr[c, n].astype(F32)
        out[:, pl.ds(CH * c, CH)] = total

    for c in range(NCH):
        remote(cs.at[c], cr.at[c], css.at[c], crs.at[c], tp=partner).wait_send()
        local(xr.at[c], xr.at[c], xss.at[c]).wait()
    local(heads_all, heads_all, ss.at[0]).wait()
    for e in range(OWN):
        sent = snd.at[e, pl.ds(0, NI - 1)]
        local(sent, sent, ss.at[2 + e]).wait()
    sent = mid2.at[pl.ds(0, OWN * (NI - 1))]
    local(sent, sent, ss.at[4]).wait()
    sent = tmid.at[pl.ds(0, OWN * (NI - 1))]
    local(sent, sent, ss.at[5]).wait()
    kept_here = 1 + jnp.where(lax.rem(zz, 2) == yy, 1, 0)
    for n_kept in (1, 2):

        @pl.when(kept_here == n_kept)
        def _():
            sent = mid.at[pl.ds(0, BLOCKS - n_kept)]
            local(sent, sent, ss.at[1]).wait()
            local(sent, sent, ss.at[6]).wait()
            sent = tsnd.at[pl.ds(0, BLOCKS - n_kept)]
            local(sent, sent, ss.at[7]).wait()


def shards(
    queries,
    row_prompt,
    owner_slot,
    suffix_len,
    prefix_keys,
    prefix_values,
    suffix_keys,
    suffix_values,
    new_keys,
    new_values,
    out_weight,
):
    smem = pl.BlockSpec(memory_space=pltpu.SMEM)
    vmem = pl.BlockSpec(memory_space=pltpu.VMEM)
    hbm = pl.BlockSpec(memory_space=pl.ANY)
    sem = pltpu.SemaphoreType.DMA
    scratch = [
        pltpu.VMEM((2, 384, HD), BF16),
        pltpu.VMEM((OWN, KEYS, HD), BF16),
        pltpu.VMEM((OWN, KEYS, 2 * HD), BF16),
        pltpu.VMEM((HALVES, 384, HD), BF16),
        pltpu.VMEM((HALVES, 384, HD), BF16),
        pltpu.VMEM((512, D), BF16),
        pltpu.VMEM((NI, 4, HD), I32),
        pltpu.VMEM((8, HD), I32),
        pltpu.SMEM((8, HD), I32),
        pltpu.VMEM((BLOCKS, 16, HD), BF16),
        pltpu.VMEM((OWN, NI, 16, HD), BF16),
        pltpu.VMEM((OWN, NI, 16, HD), BF16),
        pltpu.VMEM((256, KEYS), F32),
        pltpu.VMEM((OWN, NI, 16, HD), BF16),
        pltpu.VMEM((OWN, NI, 1, HD), F32),
        pltpu.VMEM((SLOTS, 16, HD), BF16),
        pltpu.VMEM((SLOTS, 1, HD), F32),
        pltpu.VMEM((BLOCKS, 16, HD), BF16),
        pltpu.VMEM((BLOCKS, 1, HD), F32),
        pltpu.VMEM((HALVES, NZ, 16, HD), BF16),
        pltpu.VMEM((HALVES, NZ, 1, HD), F32),
        pltpu.VMEM((HALVES, 256, HD), F32),
        pltpu.VMEM((HALVES, 256, HD), F32),
        pltpu.VMEM((HALVES, 256, HD), F32),
        pltpu.VMEM((2, 400, HD), F32),
        pltpu.VMEM((256, 512), BF16),
        pltpu.VMEM((NCH, 128, CH), F32),
        pltpu.VMEM((NCH, 128, CH), BF16),
        pltpu.VMEM((NCH, 128, CH), BF16),
        pltpu.VMEM((NCH, 8, 16, CH), BF16),
        pltpu.VMEM((NCH, 7, 16, CH), BF16),
        pltpu.VMEM((NCH, 8, 16, CH), F32),
        sem((17,)),
        sem((8,)),
        sem((8,)),
        sem((NCH,)),
        sem((NCH,)),
        sem((NCH,)),
        sem((NCH,)),
    ]
    result = pl.pallas_call(
        kernel,
        out_shape=jax.ShapeDtypeStruct((16, D), F32),
        in_specs=[smem, smem, vmem] + [hbm] * 8,
        out_specs=vmem,
        scratch_shapes=scratch,
        compiler_params=pltpu.CompilerParams(
            collective_id=0, has_side_effects=True, vmem_limit_bytes=56 * 1024 * 1024
        ),
    )(
        row_prompt,
        owner_slot,
        suffix_len.reshape(1, 96),
        queries.reshape(2, 384, HD),
        prefix_keys.reshape(OWN, KEYS, HD),
        prefix_values.reshape(OWN, KEYS, HD),
        suffix_keys.reshape(768, HD),
        suffix_values.reshape(768, HD),
        new_keys.reshape(2, 96, HD),
        new_values.reshape(2, 96, HD),
        out_weight,
    )
    rows = result.reshape(2, 8, D)[:, :6]
    return jnp.swapaxes(rows, 0, 1).astype(BF16)


def solution(mesh):
    placed = (
        P(None, "inst", "tp", None),
        P("inst"),
        P(),
        P("inst"),
        P("inst", None, "tp", None),
        P("inst", None, "tp", None),
        P("inst", None, "tp", None),
        P("inst", None, "tp", None),
        P(None, "inst", "tp", None),
        P(None, "inst", "tp", None),
        P("tp", None),
    )
    return jax.shard_map(
        shards, mesh=mesh, in_specs=placed, out_specs=P(("inst", "tp"), None, None), check_vma=False
    )
```

```python
import math

import jax
import jax.numpy as jnp
from jax import lax
from jax.experimental import pallas as pl
from jax.experimental.pallas import tpu as pltpu
from jax.sharding import PartitionSpec as P

F32 = jnp.float32
BF16 = jnp.bfloat16
I32 = jnp.int32

NI = 32
NZ = 16
HALVES = 3
BLOCKS = 48
SLOTS = 64
OWN = 2
HD = 128
KEYS = 4096
D = 2560
CH = 1280
NCH = D // CH
KC = 512
U_OF = (0, 2, 1)
SCALE = 1.0 / math.sqrt(HD)
C2 = SCALE * math.log2(math.e)
NEG = -1e30


def dot_t(a, b):
    return lax.dot_general(a, b, (((1,), (1,)), ((), ())), preferred_element_type=F32)


def dot(a, b):
    return lax.dot_general(a, b, (((1,), (0,)), ((), ())), preferred_element_type=F32)


def iota(shape, dim):
    return lax.broadcasted_iota(I32, shape, dim)


def far_first(k, n):
    up = lax.rem(k + 1, 2)
    return lax.rem(n // 2 + up * lax.div(k, 2) + (1 - up) * (n - lax.div(k + 1, 2)), n)


def kernel(
    row_prompt,
    owner_slot,
    lens,
    q_hbm,
    k_hbm,
    v_hbm,
    sk_hbm,
    sv_hbm,
    nk_hbm,
    nv_hbm,
    w_hbm,
    out,
    q,
    kk,
    va,
    ck,
    cv,
    w,
    tab,
    inv_v,
    inv_s,
    mid,
    snd,
    qin,
    scores,
    obuf,
    mid2,
    snd2,
    pin,
    tall,
    own_acc,
    own_m,
    own_l,
    att,
    lhs,
    mine,
    cs,
    cr,
    xs,
    xr,
    sums,
    ld,
    ss,
    rs,
    css,
    crs,
    xss,
    xrs,
):
    inst = lax.axis_index("inst")
    tp = lax.axis_index("tp")
    yy = lax.div(inst, NZ)
    zz = lax.rem(inst, NZ)
    core = lax.rem(tp, 2)
    chip = lax.div(tp, 2)
    partner = tp + 1 - 2 * core
    my_t = lax.rem(zz, 2)
    my_m = lax.div(zz, 2)

    def remote(src, dst, s, r, **where):
        return pltpu.make_async_remote_copy(
            src_ref=src, dst_ref=dst, send_sem=s, recv_sem=r,
            device_id=where, device_id_type=pl.DeviceIdType.MESH,
        )

    def local(src, dst, s):
        return pltpu.make_async_copy(src, dst, s)

    def chip_at(step):
        return lax.rem(chip + step, 8) * 2 + core

    left = []

    def left_of(ref, sem):
        left.append(lambda: local(ref, ref, sem).wait())

    loads_q = [
        local(q_hbm.at[:, pl.ds(128 * U_OF[o], 128)], q.at[:, o], ld.at[0]) for o in range(HALVES)
    ]
    for c in loads_q:
        c.start()
    loads_own = []
    for o in range(HALVES):
        u = U_OF[o]
        for src, dst, sem in ((sk_hbm, ck, 3), (sv_hbm, cv, 4)):
            loads_own.append(
                local(src.at[pl.ds(256 * u, 256)], dst.at[o, pl.ds(0, 256)], ld.at[sem + 4 * o])
            )
        for src, dst, sem in ((nk_hbm, ck, 5), (nv_hbm, cv, 6)):
            loads_own.append(
                local(
                    src.at[:, pl.ds(32 * u, 32)],
                    dst.at[o, pl.ds(256, 64)].reshape(2, 32, HD),
                    ld.at[sem + 4 * o],
                )
            )
    for c in loads_own:
        c.start()
    load_k = local(k_hbm, kk, ld.at[1])
    load_k.start()
    load_v = local(v_hbm, va.at[:, :, pl.ds(0, HD)], ld.at[2])
    load_v.start()
    load_w = local(w_hbm, w, ld.at[15])
    load_w.start()

    barrier = pltpu.get_barrier_semaphore()

    def greet(k, _):
        z = lax.rem(zz + far_first(k, NZ), NZ)
        for y in (1 - yy, yy):
            pl.semaphore_signal(
                barrier, inc=1, device_id={"inst": y * NZ + z},
                device_id_type=pl.DeviceIdType.MESH,
            )
        return 0

    lax.fori_loop(0, NZ - 1, greet, 0)
    pl.semaphore_signal(
        barrier, inc=1, device_id={"inst": (1 - yy) * NZ + zz}, device_id_type=pl.DeviceIdType.MESH
    )

    def greet_chip(n, _):
        pl.semaphore_signal(
            barrier, inc=1, device_id={"tp": chip_at(n)}, device_id_type=pl.DeviceIdType.MESH
        )
        return 0

    lax.fori_loop(1, 8, greet_chip, 0)
    pl.semaphore_signal(
        barrier, inc=1, device_id={"tp": partner}, device_id_type=pl.DeviceIdType.MESH
    )

    lane1 = iota((1, HD), 1)
    head = jnp.zeros((1, HD), I32)
    for u in range(HALVES):
        block = lax.div(HALVES * inst + u, 2)
        first = lax.rem(HALVES * inst + u, 2) == 0
        slot = owner_slot[row_prompt[32 * u]]
        head += jnp.where((lane1 == slot) & first, block, 0)
        head += jnp.where((lane1 == SLOTS + block) & first, slot, 0)
    tab[inst] = head
    ones = jnp.ones((256, HD), BF16)

    def set_ones(n, _):
        va[lax.div(n, 16), pl.ds(pl.multiple_of(lax.rem(n, 16) * 256, 256), 256), pl.ds(HD, HD)] = ones
        return 0

    lax.fori_loop(0, 32, set_ones, 0)
    for o in range(HALVES):
        ck[o, pl.ds(320, 64)] = jnp.zeros((64, HD), BF16)
        cv[o, pl.ds(320, 64)] = jnp.zeros((64, HD), BF16)
    for c in loads_q:
        c.wait()

    pl.semaphore_wait(barrier, NI - 1 + 1 + 7)

    b_outer = lax.div(HALVES * inst, 2)
    b_inner = lax.div(HALVES * inst + 1, 2)
    side_outer = lax.rem(zz, 2)
    side_inner = 1 - side_outer

    def outer_piece(z):
        at = pl.ds(pl.multiple_of(16 * lax.div(z, 2), 16), 16)
        return q.at[lax.rem(z, 2), pl.ds(0, 2), at], mid.at[pl.ds(b_outer, 2)]

    def inner_piece(z):
        at = pl.ds(pl.multiple_of(16 * lax.div(z, 2), 16), 16)
        return q.at[lax.rem(z, 2), 2, at], mid.at[b_inner]

    def send_head(d):
        remote(tab.at[inst], tab.at[inst], ss.at[0], rs.at[0], inst=d).start()

    def send_piece(k, _):
        z = lax.rem(zz + far_first(k, NZ), NZ)
        send_head(side_outer * NZ + z)
        send_head(side_inner * NZ + z)
        remote(*outer_piece(z), ss.at[1], rs.at[1], inst=side_outer * NZ + z).start()
        remote(*inner_piece(z), ss.at[1], rs.at[1], inst=side_inner * NZ + z).start()
        return 0

    lax.fori_loop(0, NZ - 1, send_piece, 0)
    across = (1 - yy) * NZ + zz
    send_head(across)

    @pl.when(side_outer == yy)
    def _():
        local(*outer_piece(zz), rs.at[1]).start()
        remote(*inner_piece(zz), ss.at[1], rs.at[1], inst=across).start()

    @pl.when(side_outer != yy)
    def _():
        local(*inner_piece(zz), rs.at[1]).start()
        remote(*outer_piece(zz), ss.at[1], rs.at[1], inst=across).start()

    heads_all = tab.at[pl.ds(0, NI - 1)]
    left_of(heads_all, ss.at[0])
    kept_here = 1 + jnp.where(side_outer == yy, 1, 0)

    def left_halves(ref, sem):
        def wait():
            for n_kept in (1, 2):

                @pl.when(kept_here == n_kept)
                def _():
                    sent = ref.at[pl.ds(0, BLOCKS - n_kept)]
                    local(sent, sent, sem).wait()

        left.append(wait)

    left_halves(mid, ss.at[1])

    for c in loads_own:
        c.wait()
    lens_b = jnp.broadcast_to(lens[...].astype(F32), (8, 96)).astype(BF16)
    for o in range(HALVES):
        u = U_OF[o]
        at96 = iota((96, 384), 0)
        lane96 = iota((96, 384), 1)
        spread = jnp.where(at96 == 32 * u + lax.div(lane96, 8), 1.0, 0.0).astype(BF16)
        len_row = dot(lens_b, spread)[0:1]
        row = iota((256, 384), 0)
        lane = iota((256, 384), 1)
        sample = lax.div(lax.rem(row, 128), 4)
        step = lax.div(row, 128)
        cached = (lane < 256) & (lax.div(lane, 8) == sample) & (
            lax.rem(lane, 8).astype(F32) < jnp.broadcast_to(len_row, (256, 384))
        )
        new_at = lane - 256
        new = (lane >= 256) & (lane < 320) & (lax.rem(new_at, 32) == sample) & (
            lax.div(new_at, 32) <= step
        )
        qu = jnp.concatenate([q[0, o], q[1, o]], axis=0)
        s = jnp.where(cached | new, dot_t(qu, ck[o]), NEG)
        top = jnp.max(s, axis=1, keepdims=True)
        p = jnp.exp2(s * C2 - top * C2)
        own_m[o] = jnp.broadcast_to(top * SCALE, (256, HD))
        own_l[o] = jnp.broadcast_to(jnp.sum(p, axis=1, keepdims=True), (256, HD))
        own_acc[o] = dot(p.astype(BF16), cv[o])

    local(heads_all, heads_all, rs.at[0]).wait()
    inv_v[...] = jnp.sum(tab[...], axis=0)
    to_smem = local(inv_v, inv_s, ld.at[16])
    to_smem.start()
    to_smem.wait()

    def slot_block(s):
        return jnp.clip(inv_s[0, s], 0, BLOCKS - 1)

    def block_slot(n):
        return jnp.clip(inv_s[0, SLOTS + n], 0, SLOTS - 1)

    local(mid, mid, rs.at[1]).wait()

    def select(d):
        for e in range(OWN):
            snd[d, e] = mid[slot_block(OWN * d + e)]

    def to_owner(d):
        return remote(snd.at[d], qin.at[my_t, yy, my_m], ss.at[2], rs.at[2 + my_t], inst=d)

    def send_selected(k, _):
        z = lax.rem(zz + far_first(k, NZ), NZ)
        for y in (1 - yy, yy):
            d = y * NZ + z
            select(d)
            to_owner(d).start()
        return 0

    lax.fori_loop(0, NZ - 1, send_selected, 0)
    select(across)
    to_owner(across).start()
    select(inst)
    local(snd.at[inst], qin.at[my_t, yy, my_m], rs.at[2 + my_t]).start()
    left_of(snd.at[pl.ds(0, NI - 1)], ss.at[2])

    load_k.wait()
    load_v.wait()
    eye = iota((HD, HD), 0) == iota((HD, HD), 1)
    for t in range(2):
        local(qin.at[t], qin.at[t], rs.at[2 + t]).wait()
        for e in range(OWN):
            qv = qin[t, :, :, e].reshape(256, HD)
            top = None
            for c in range(KEYS // KC):
                s = dot_t(qv, kk[e, pl.ds(KC * c, KC)])
                scores[:, pl.ds(KC * c, KC)] = s
                for j in range(KC // HD):
                    part = s[:, HD * j : HD * (j + 1)]
                    top = part if top is None else jnp.maximum(top, part)
            top = jnp.max(top, axis=1, keepdims=True)
            shift = top * C2
            acc = jnp.zeros((256, 2 * HD), F32)
            for c in range(KEYS // KC):
                p = jnp.exp2(scores[:, pl.ds(KC * c, KC)] * C2 - shift)
                acc += dot(p.astype(BF16), va[e, pl.ds(KC * c, KC)])
            weight = acc[:, HD:]
            obuf[t, :, :, e] = (acc[:, :HD] / weight).astype(BF16).reshape(2, 8, 16, HD)
            total = top * SCALE + jnp.log(weight)
            for y in range(2):
                tall[8 * inst + 4 * e + 2 * t + y] = jnp.sum(
                    jnp.where(eye, total[HD * y : HD * (y + 1)], 0.0), axis=0, keepdims=True
                )
        base = lax.rem(zz + lax.rem(zz + t, 2), NZ)
        slots = mid2.at[pl.ds(OWN * inst, OWN)]

        def back(k, _):
            z = lax.rem(base + 2 * far_first(k, 8), NZ)
            for y in (1 - yy, yy):
                remote(
                    obuf.at[t, y, lax.div(z, 2)], slots, ss.at[4], rs.at[4], inst=y * NZ + z
                ).start()
            return 0

        lax.fori_loop(0, 7, back, 0)
        near = lax.div(base, 2)
        remote(
            obuf.at[t, 1 - yy, near], slots, ss.at[4], rs.at[4], inst=(1 - yy) * NZ + base
        ).start()

        @pl.when(my_t == t)
        def _():
            local(obuf.at[t, yy, near], slots, rs.at[4]).start()

        @pl.when(my_t != t)
        def _():
            remote(obuf.at[t, yy, near], slots, ss.at[4], rs.at[4], inst=yy * NZ + base).start()

    left_of(mid2.at[pl.ds(0, OWN * (NI - 1))], ss.at[4])

    def send_totals(d):
        mine8 = tall.at[pl.ds(8 * inst, 8)]
        remote(mine8, mine8, ss.at[5], rs.at[5], inst=d).start()

    def spread_totals(k, _):
        z = lax.rem(zz + far_first(k, NZ), NZ)
        for y in (1 - yy, yy):
            send_totals(y * NZ + z)
        return 0

    lax.fori_loop(0, NZ - 1, spread_totals, 0)
    send_totals(across)
    totals_all = tall.at[pl.ds(0, 8 * (NI - 1))]
    left_of(totals_all, ss.at[5])

    local(mid2, mid2, rs.at[4]).wait()

    def select2(n, _):
        snd2[n] = mid2[block_slot(n)]
        return 0

    lax.fori_loop(0, BLOCKS, select2, 0)

    def home(d, kept):
        outer = snd2.at[pl.ds(lax.div(HALVES * d, 2), 2)], pin.at[my_t, my_m, pl.ds(0, 2)]
        inner = snd2.at[lax.div(HALVES * d + 1, 2)], pin.at[my_t, my_m, 2]
        for refs, parity in ((outer, 0), (inner, 1)):

            @pl.when(lax.rem(d + yy, 2) == parity)
            def _():
                if kept:
                    local(*refs, rs.at[6 + my_t]).start()
                else:
                    remote(*refs, ss.at[6], rs.at[6 + my_t], inst=d).start()

    def send_home(k, _):
        z = lax.rem(zz + far_first(k, NZ), NZ)
        for y in (1 - yy, yy):
            home(y * NZ + z, False)
        return 0

    lax.fori_loop(0, NZ - 1, send_home, 0)
    home(across, False)
    home(inst, True)
    left_halves(snd2, ss.at[6])

    load_w.wait()
    local(totals_all, totals_all, rs.at[5]).wait()
    kept = pl.ds(pl.multiple_of(core * 64, 64), 64)
    given = pl.ds(pl.multiple_of((1 - core) * 64, 64), 64)
    for t in range(2):
        local(pin.at[t], pin.at[t], rs.at[6 + t]).wait()
        for o in range(HALVES):
            slot = block_slot(lax.div(HALVES * inst + U_OF[o], 2))
            side = side_inner if o == 2 else side_outer
            vec = tall[slot * 4 + 2 * t + side]
            total = jnp.sum(
                jnp.where(eye, jnp.broadcast_to(vec, (HD, HD)), 0.0), axis=1, keepdims=True
            )
            rows = pl.ds(HD * t, HD)
            own_top = own_m[o, rows]
            top = jnp.maximum(total, own_top)
            carried = jnp.exp(total - top)
            own = jnp.exp(own_top - top)
            below = carried + own * own_l[o, rows]
            before = pin[t, :, o].reshape(HD, HD).astype(F32)
            att[t, pl.ds(HD * U_OF[o], HD)] = (carried * before + own * own_acc[o, rows]) / below
        att[t, pl.ds(384, 16)] = jnp.zeros((16, HD), F32)
        for c in range(2):
            for a in range(0, 8, 2):
                for h in range(4):
                    pair = [att[t, pl.ds(24 * (2 * b + c) + h, 8, stride=4)] for b in (a, a + 1)]
                    lhs[t, pl.ds(64 * c + 8 * a, 16), pl.ds(HD * h, HD)] = jnp.concatenate(
                        pair, axis=0
                    ).astype(BF16)
        for c in range(NCH):
            cs[t, c] = dot(lhs[t, given], w[:, pl.ds(CH * c, CH)]).astype(BF16)
            remote(
                cs.at[t, c], cr.at[t, c], css.at[2 * t + c], crs.at[2 * t + c], tp=partner
            ).start()
        for c in range(NCH):
            mine[c] = dot(lhs[t, kept], w[:, pl.ds(CH * c, CH)])
        for c in range(NCH):
            pair_copy = remote(
                cs.at[t, c], cr.at[t, c], css.at[2 * t + c], crs.at[2 * t + c], tp=partner
            )
            pair_copy.wait_recv()
            left.append(pair_copy.wait_send)
            both = (mine[c] + cr[t, c].astype(F32)).reshape(8, 8, CH)
            both = jnp.concatenate([both[:, :, : CH // 2], both[:, :, CH // 2 :]], axis=1)
            sums[t, c] = both
            xs[t, c] = both.astype(BF16)

            def spread_out(n, _):
                remote(
                    xs.at[t, c, lax.rem(chip + n, 8)],
                    xr.at[t, c, n - 1],
                    xss.at[2 * t + c],
                    xrs.at[2 * t + c],
                    tp=chip_at(n),
                ).start()
                return 0

            lax.fori_loop(1, 8, spread_out, 0)
            left_of(xr.at[t, c], xss.at[2 * t + c])
    for t in range(2):
        for c in range(NCH):
            local(xr.at[t, c], xr.at[t, c], xrs.at[2 * t + c]).wait()
            total = sums[t, c, chip]
            for n in range(7):
                total = total + xr[t, c, n].astype(F32)
            out[t, :, pl.ds(CH * c, CH // 2)] = total[:8]
            out[t, :, pl.ds(CH * c + CH // 2, CH // 2)] = total[8:]

    for wait in left:
        wait()


def shards(
    queries,
    row_prompt,
    owner_slot,
    suffix_len,
    prefix_keys,
    prefix_values,
    suffix_keys,
    suffix_values,
    new_keys,
    new_values,
    out_weight,
):
    smem = pl.BlockSpec(memory_space=pltpu.SMEM)
    vmem = pl.BlockSpec(memory_space=pltpu.VMEM)
    hbm = pl.BlockSpec(memory_space=pl.ANY)
    sem = pltpu.SemaphoreType.DMA
    scratch = [
        pltpu.VMEM((2, HALVES, 128, HD), BF16),
        pltpu.VMEM((OWN, KEYS, HD), BF16),
        pltpu.VMEM((OWN, KEYS, 2 * HD), BF16),
        pltpu.VMEM((HALVES, 384, HD), BF16),
        pltpu.VMEM((HALVES, 384, HD), BF16),
        pltpu.VMEM((512, D), BF16),
        pltpu.VMEM((NI, 1, HD), I32),
        pltpu.VMEM((1, HD), I32),
        pltpu.SMEM((1, HD), I32),
        pltpu.VMEM((BLOCKS, 16, HD), BF16),
        pltpu.VMEM((NI, OWN, 16, HD), BF16),
        pltpu.VMEM((2, 2, 8, OWN, 16, HD), BF16),
        pltpu.VMEM((256, KEYS), F32),
        pltpu.VMEM((2, 2, 8, OWN, 16, HD), BF16),
        pltpu.VMEM((SLOTS, 16, HD), BF16),
        pltpu.VMEM((BLOCKS, 16, HD), BF16),
        pltpu.VMEM((2, 8, HALVES, 16, HD), BF16),
        pltpu.VMEM((NI * 8, 1, HD), F32),
        pltpu.VMEM((HALVES, 256, HD), F32),
        pltpu.VMEM((HALVES, 256, HD), F32),
        pltpu.VMEM((HALVES, 256, HD), F32),
        pltpu.VMEM((2, 400, HD), F32),
        pltpu.VMEM((2, 128, 512), BF16),
        pltpu.VMEM((NCH, 64, CH), F32),
        pltpu.VMEM((2, NCH, 64, CH), BF16),
        pltpu.VMEM((2, NCH, 64, CH), BF16),
        pltpu.VMEM((2, NCH, 8, 16, CH // 2), BF16),
        pltpu.VMEM((2, NCH, 7, 16, CH // 2), BF16),
        pltpu.VMEM((2, NCH, 8, 16, CH // 2), F32),
        sem((17,)),
        sem((8,)),
        sem((8,)),
        sem((2 * NCH,)),
        sem((2 * NCH,)),
        sem((2 * NCH,)),
        sem((2 * NCH,)),
    ]
    result = pl.pallas_call(
        kernel,
        out_shape=jax.ShapeDtypeStruct((2, 8, D), F32),
        in_specs=[smem, smem, vmem] + [hbm] * 8,
        out_specs=vmem,
        scratch_shapes=scratch,
        compiler_params=pltpu.CompilerParams(
            collective_id=0, has_side_effects=True, vmem_limit_bytes=56 * 1024 * 1024
        ),
    )(
        row_prompt,
        owner_slot,
        suffix_len.reshape(1, 96),
        queries.reshape(2, 384, HD),
        prefix_keys.reshape(OWN, KEYS, HD),
        prefix_values.reshape(OWN, KEYS, HD),
        suffix_keys.reshape(768, HD),
        suffix_values.reshape(768, HD),
        new_keys.reshape(2, 96, HD),
        new_values.reshape(2, 96, HD),
        out_weight,
    )
    rows = result[:, :6]
    return jnp.swapaxes(rows, 0, 1).astype(BF16)


def solution(mesh):
    placed = (
        P(None, "inst", "tp", None),
        P("inst"),
        P(),
        P("inst"),
        P("inst", None, "tp", None),
        P("inst", None, "tp", None),
        P("inst", None, "tp", None),
        P("inst", None, "tp", None),
        P(None, "inst", "tp", None),
        P(None, "inst", "tp", None),
        P("tp", None),
    )
    return jax.shard_map(
        shards, mesh=mesh, in_specs=placed, out_specs=P(("inst", "tp"), None, None), check_vma=False
    )
```

```python
import math

import jax
import jax.numpy as jnp
from jax import lax
from jax.experimental import pallas as pl
from jax.experimental.pallas import tpu as pltpu
from jax.sharding import PartitionSpec as P

F32 = jnp.float32
BF16 = jnp.bfloat16
I32 = jnp.int32

NI = 32
NZ = 16
HALVES = 3
BLOCKS = 48
SLOTS = 64
OWN = 2
HD = 128
KEYS = 4096
D = 2560
CH = 1280
NCH = D // CH
KC = 1024
U_OF = (0, 2, 1)
SCALE = 1.0 / math.sqrt(HD)
C2 = SCALE * math.log2(math.e)
NEG = -1e30


def dot_t(a, b):
    return lax.dot_general(a, b, (((1,), (1,)), ((), ())), preferred_element_type=F32)


def dot(a, b):
    return lax.dot_general(a, b, (((1,), (0,)), ((), ())), preferred_element_type=F32)


def iota(shape, dim):
    return lax.broadcasted_iota(I32, shape, dim)


def far_first(k, n):
    up = lax.rem(k + 1, 2)
    return lax.rem(n // 2 + up * lax.div(k, 2) + (1 - up) * (n - lax.div(k + 1, 2)), n)


def kernel(
    row_prompt,
    owner_slot,
    lens,
    q_hbm,
    k_hbm,
    v_hbm,
    sk_hbm,
    sv_hbm,
    nk_hbm,
    nv_hbm,
    w_hbm,
    out,
    q,
    kk,
    va,
    ck,
    cv,
    w,
    tab,
    inv_v,
    inv_s,
    mid,
    snd,
    qin,
    obuf,
    mid2,
    snd2,
    pin,
    tall,
    own_acc,
    own_m,
    own_l,
    att,
    lhs,
    mine,
    cs,
    cr,
    xs,
    xr,
    sums,
    ld,
    ss,
    rs,
    css,
    crs,
    xss,
    xrs,
):
    inst = lax.axis_index("inst")
    tp = lax.axis_index("tp")
    yy = lax.div(inst, NZ)
    zz = lax.rem(inst, NZ)
    core = lax.rem(tp, 2)
    chip = lax.div(tp, 2)
    partner = tp + 1 - 2 * core
    my_t = lax.rem(zz, 2)
    my_m = lax.div(zz, 2)

    def remote(src, dst, s, r, **where):
        return pltpu.make_async_remote_copy(
            src_ref=src, dst_ref=dst, send_sem=s, recv_sem=r,
            device_id=where, device_id_type=pl.DeviceIdType.MESH,
        )

    def local(src, dst, s):
        return pltpu.make_async_copy(src, dst, s)

    def chip_at(step):
        return lax.rem(chip + step, 8) * 2 + core

    left = []

    def left_of(ref, sem):
        left.append(lambda: local(ref, ref, sem).wait())

    loads_q = [
        local(q_hbm.at[:, pl.ds(128 * U_OF[o], 128)], q.at[:, o], ld.at[0]) for o in range(HALVES)
    ]
    for c in loads_q:
        c.start()
    loads_own = []
    for o in range(HALVES):
        u = U_OF[o]
        for src, dst, sem in ((sk_hbm, ck, 3), (sv_hbm, cv, 4)):
            loads_own.append(
                local(src.at[pl.ds(256 * u, 256)], dst.at[o, pl.ds(0, 256)], ld.at[sem + 4 * o])
            )
        for src, dst, sem in ((nk_hbm, ck, 5), (nv_hbm, cv, 6)):
            loads_own.append(
                local(
                    src.at[:, pl.ds(32 * u, 32)],
                    dst.at[o, pl.ds(256, 64)].reshape(2, 32, HD),
                    ld.at[sem + 4 * o],
                )
            )
    for c in loads_own:
        c.start()
    load_k = local(k_hbm, kk, ld.at[1])
    load_k.start()
    load_v = local(v_hbm, va.at[:, :, pl.ds(0, HD)], ld.at[2])
    load_v.start()
    load_w = local(w_hbm, w, ld.at[15])
    load_w.start()

    barrier = pltpu.get_barrier_semaphore()

    def greet(k, _):
        z = lax.rem(zz + far_first(k, NZ), NZ)
        for y in (1 - yy, yy):
            pl.semaphore_signal(
                barrier, inc=1, device_id={"inst": y * NZ + z},
                device_id_type=pl.DeviceIdType.MESH,
            )
        return 0

    lax.fori_loop(0, NZ - 1, greet, 0)
    pl.semaphore_signal(
        barrier, inc=1, device_id={"inst": (1 - yy) * NZ + zz}, device_id_type=pl.DeviceIdType.MESH
    )

    def greet_chip(n, _):
        pl.semaphore_signal(
            barrier, inc=1, device_id={"tp": chip_at(n)}, device_id_type=pl.DeviceIdType.MESH
        )
        return 0

    lax.fori_loop(1, 8, greet_chip, 0)
    pl.semaphore_signal(
        barrier, inc=1, device_id={"tp": partner}, device_id_type=pl.DeviceIdType.MESH
    )

    lane1 = iota((1, HD), 1)
    head = jnp.zeros((1, HD), I32)
    for u in range(HALVES):
        block = lax.div(HALVES * inst + u, 2)
        first = lax.rem(HALVES * inst + u, 2) == 0
        slot = owner_slot[row_prompt[32 * u]]
        head += jnp.where((lane1 == slot) & first, block, 0)
        head += jnp.where((lane1 == SLOTS + block) & first, slot, 0)
    tab[inst] = head
    ones = jnp.ones((256, HD), BF16)

    def set_ones(n, _):
        va[lax.div(n, 16), pl.ds(pl.multiple_of(lax.rem(n, 16) * 256, 256), 256), pl.ds(HD, HD)] = ones
        return 0

    lax.fori_loop(0, 32, set_ones, 0)
    for o in range(HALVES):
        ck[o, pl.ds(320, 64)] = jnp.zeros((64, HD), BF16)
        cv[o, pl.ds(320, 64)] = jnp.zeros((64, HD), BF16)
    for c in loads_q:
        c.wait()

    pl.semaphore_wait(barrier, NI - 1 + 1 + 7)

    b_outer = lax.div(HALVES * inst, 2)
    b_inner = lax.div(HALVES * inst + 1, 2)
    side_outer = lax.rem(zz, 2)
    side_inner = 1 - side_outer

    def outer_piece(z):
        at = pl.ds(pl.multiple_of(16 * lax.div(z, 2), 16), 16)
        return q.at[lax.rem(z, 2), pl.ds(0, 2), at], mid.at[pl.ds(b_outer, 2)]

    def inner_piece(z):
        at = pl.ds(pl.multiple_of(16 * lax.div(z, 2), 16), 16)
        return q.at[lax.rem(z, 2), 2, at], mid.at[b_inner]

    def send_head(d):
        remote(tab.at[inst], tab.at[inst], ss.at[0], rs.at[0], inst=d).start()

    def send_pieces(z):
        send_head(side_outer * NZ + z)
        send_head(side_inner * NZ + z)
        remote(*outer_piece(z), ss.at[1], rs.at[1], inst=side_outer * NZ + z).start()
        remote(*inner_piece(z), ss.at[1], rs.at[1], inst=side_inner * NZ + z).start()

    bases = [lax.rem(zz + lax.rem(zz + t, 2), NZ) for t in range(2)]
    across = (1 - yy) * NZ + zz
    for t in range(2):

        def send_step(k, _):
            send_pieces(lax.rem(bases[t] + 2 * far_first(k, 8), NZ))
            return 0

        lax.fori_loop(0, 7, send_step, 0)

        @pl.when(my_t != t)
        def _():
            send_pieces(bases[t])

        @pl.when((my_t == t) & (side_outer == yy))
        def _():
            send_head(across)
            local(*outer_piece(zz), rs.at[1]).start()
            remote(*inner_piece(zz), ss.at[1], rs.at[1], inst=across).start()

        @pl.when((my_t == t) & (side_outer != yy))
        def _():
            send_head(across)
            local(*inner_piece(zz), rs.at[1]).start()
            remote(*outer_piece(zz), ss.at[1], rs.at[1], inst=across).start()

    heads_all = tab.at[pl.ds(0, NI - 1)]
    left_of(heads_all, ss.at[0])
    kept_here = 1 + jnp.where(side_outer == yy, 1, 0)

    def left_halves(ref, sem):
        def wait():
            for n_kept in (1, 2):

                @pl.when(kept_here == n_kept)
                def _():
                    sent = ref.at[pl.ds(0, BLOCKS - n_kept)]
                    local(sent, sent, sem).wait()

        left.append(wait)

    left_halves(mid, ss.at[1])

    for c in loads_own:
        c.wait()
    lens_b = jnp.broadcast_to(lens[...].astype(F32), (8, 96)).astype(BF16)
    for o in range(HALVES):
        u = U_OF[o]
        at96 = iota((96, 384), 0)
        lane96 = iota((96, 384), 1)
        spread = jnp.where(at96 == 32 * u + lax.div(lane96, 8), 1.0, 0.0).astype(BF16)
        len_row = dot(lens_b, spread)[0:1]
        row = iota((256, 384), 0)
        lane = iota((256, 384), 1)
        sample = lax.div(lax.rem(row, 128), 4)
        step = lax.div(row, 128)
        cached = (lane < 256) & (lax.div(lane, 8) == sample) & (
            lax.rem(lane, 8).astype(F32) < jnp.broadcast_to(len_row, (256, 384))
        )
        new_at = lane - 256
        new = (lane >= 256) & (lane < 320) & (lax.rem(new_at, 32) == sample) & (
            lax.div(new_at, 32) <= step
        )
        qu = jnp.concatenate([q[0, o], q[1, o]], axis=0)
        s = jnp.where(cached | new, dot_t(qu, ck[o]), NEG)
        top = jnp.max(s, axis=1, keepdims=True)
        p = jnp.exp2(s * C2 - top * C2)
        own_m[o] = jnp.broadcast_to(top * SCALE, (256, HD))
        own_l[o] = jnp.broadcast_to(jnp.sum(p, axis=1, keepdims=True), (256, HD))
        own_acc[o] = dot(p.astype(BF16), cv[o])

    local(heads_all, heads_all, rs.at[0]).wait()
    inv_v[...] = jnp.sum(tab[...], axis=0)
    to_smem = local(inv_v, inv_s, ld.at[16])
    to_smem.start()
    to_smem.wait()

    def slot_block(s):
        return jnp.clip(inv_s[0, s], 0, BLOCKS - 1)

    def block_slot(n):
        return jnp.clip(inv_s[0, SLOTS + n], 0, SLOTS - 1)

    local(mid, mid, rs.at[1]).wait()

    def select(d):
        for e in range(OWN):
            snd[d, e] = mid[slot_block(OWN * d + e)]

    def to_owner(d):
        return remote(snd.at[d], qin.at[my_t, yy, my_m], ss.at[2], rs.at[2 + my_t], inst=d)

    def send_selected(k, _):
        z = lax.rem(zz + far_first(k, NZ), NZ)
        for y in (1 - yy, yy):
            d = y * NZ + z
            select(d)
            to_owner(d).start()
        return 0

    lax.fori_loop(0, NZ - 1, send_selected, 0)
    select(across)
    to_owner(across).start()
    select(inst)
    local(snd.at[inst], qin.at[my_t, yy, my_m], rs.at[2 + my_t]).start()
    left_of(snd.at[pl.ds(0, NI - 1)], ss.at[2])

    load_k.wait()
    load_v.wait()
    eye = iota((HD, HD), 0) == iota((HD, HD), 1)
    for t in range(2):
        local(qin.at[t], qin.at[t], rs.at[2 + t]).wait()
        for e in range(OWN):
            qv = qin[t, :, :, e].reshape(256, HD)
            top = jnp.full((256, 1), NEG, F32)
            acc = jnp.zeros((256, 2 * HD), F32)
            for c in range(KEYS // KC):
                s = dot_t(qv, kk[e, pl.ds(KC * c, KC)])
                part = s[:, :HD]
                for j in range(1, KC // HD):
                    part = jnp.maximum(part, s[:, HD * j : HD * (j + 1)])
                higher = jnp.maximum(top, jnp.max(part, axis=1, keepdims=True))
                p = jnp.exp2(s * C2 - higher * C2)
                again = jnp.exp2((top - higher) * C2)
                acc = acc * again + dot(p.astype(BF16), va[e, pl.ds(KC * c, KC)])
                top = higher
            weight = acc[:, HD:]
            obuf[t, :, :, e] = (acc[:, :HD] / weight).astype(BF16).reshape(2, 8, 16, HD)
            total = top * SCALE + jnp.log(weight)
            for y in range(2):
                tall[8 * inst + 4 * e + 2 * t + y] = jnp.sum(
                    jnp.where(eye, total[HD * y : HD * (y + 1)], 0.0), axis=0, keepdims=True
                )
        base = bases[t]
        slots = mid2.at[pl.ds(OWN * inst, OWN)]

        def back(k, _):
            z = lax.rem(base + 2 * far_first(k, 8), NZ)
            for y in (1 - yy, yy):
                remote(
                    obuf.at[t, y, lax.div(z, 2)], slots, ss.at[4], rs.at[4], inst=y * NZ + z
                ).start()
            return 0

        lax.fori_loop(0, 7, back, 0)
        near = lax.div(base, 2)
        remote(
            obuf.at[t, 1 - yy, near], slots, ss.at[4], rs.at[4], inst=(1 - yy) * NZ + base
        ).start()

        @pl.when(my_t == t)
        def _():
            local(obuf.at[t, yy, near], slots, rs.at[4]).start()

        @pl.when(my_t != t)
        def _():
            remote(obuf.at[t, yy, near], slots, ss.at[4], rs.at[4], inst=yy * NZ + base).start()

    left_of(mid2.at[pl.ds(0, OWN * (NI - 1))], ss.at[4])

    def send_totals(d):
        mine8 = tall.at[pl.ds(8 * inst, 8)]
        remote(mine8, mine8, ss.at[5], rs.at[5], inst=d).start()

    def spread_totals(k, _):
        z = lax.rem(zz + far_first(k, NZ), NZ)
        for y in (1 - yy, yy):
            send_totals(y * NZ + z)
        return 0

    lax.fori_loop(0, NZ - 1, spread_totals, 0)
    send_totals(across)
    totals_all = tall.at[pl.ds(0, 8 * (NI - 1))]
    left_of(totals_all, ss.at[5])

    local(mid2, mid2, rs.at[4]).wait()

    def select2(n, _):
        snd2[n] = mid2[block_slot(n)]
        return 0

    lax.fori_loop(0, BLOCKS, select2, 0)

    def home(d, kept):
        outer = snd2.at[pl.ds(lax.div(HALVES * d, 2), 2)], pin.at[my_t, my_m, pl.ds(0, 2)]
        inner = snd2.at[lax.div(HALVES * d + 1, 2)], pin.at[my_t, my_m, 2]
        for refs, parity in ((outer, 0), (inner, 1)):

            @pl.when(lax.rem(d + yy, 2) == parity)
            def _():
                if kept:
                    local(*refs, rs.at[6 + my_t]).start()
                else:
                    remote(*refs, ss.at[6], rs.at[6 + my_t], inst=d).start()

    def send_home(k, _):
        z = lax.rem(zz + far_first(k, NZ), NZ)
        for y in (1 - yy, yy):
            home(y * NZ + z, False)
        return 0

    lax.fori_loop(0, NZ - 1, send_home, 0)
    home(across, False)
    home(inst, True)
    left_halves(snd2, ss.at[6])

    load_w.wait()
    local(totals_all, totals_all, rs.at[5]).wait()
    for t in range(2):
        local(pin.at[t], pin.at[t], rs.at[6 + t]).wait()
        for o in range(HALVES):
            slot = block_slot(lax.div(HALVES * inst + U_OF[o], 2))
            side = side_inner if o == 2 else side_outer
            vec = tall[slot * 4 + 2 * t + side]
            total = jnp.sum(
                jnp.where(eye, jnp.broadcast_to(vec, (HD, HD)), 0.0), axis=1, keepdims=True
            )
            rows = pl.ds(HD * t, HD)
            own_top = own_m[o, rows]
            top = jnp.maximum(total, own_top)
            carried = jnp.exp(total - top)
            own = jnp.exp(own_top - top)
            below = carried + own * own_l[o, rows]
            before = pin[t, :, o].reshape(HD, HD).astype(F32)
            att[t, pl.ds(HD * U_OF[o], HD)] = (carried * before + own * own_acc[o, rows]) / below
        att[t, pl.ds(384, 16)] = jnp.zeros((16, HD), F32)
        for c in range(2):
            for a in range(0, 8, 2):
                for h in range(4):
                    pair = [att[t, pl.ds(24 * (2 * b + c) + h, 8, stride=4)] for b in (a, a + 1)]
                    lhs[t, pl.ds(64 * c + 8 * a, 16), pl.ds(HD * h, HD)] = jnp.concatenate(
                        pair, axis=0
                    ).astype(BF16)
        for c in range(NCH):
            part = dot(lhs[t], w[:, pl.ds(CH * c, CH)])
            cs[t, c] = jnp.where(core == 0, part[64:], part[:64]).astype(BF16)
            mine[t, c] = jnp.where(core == 0, part[:64], part[64:])
            remote(
                cs.at[t, c], cr.at[t, c], css.at[2 * t + c], crs.at[2 * t + c], tp=partner
            ).start()
        for c in range(NCH):
            pair_copy = remote(
                cs.at[t, c], cr.at[t, c], css.at[2 * t + c], crs.at[2 * t + c], tp=partner
            )
            pair_copy.wait_recv()
            left.append(pair_copy.wait_send)
            both = (mine[t, c] + cr[t, c].astype(F32)).reshape(8, 8, CH)
            both = jnp.concatenate([both[:, :, : CH // 2], both[:, :, CH // 2 :]], axis=1)
            sums[t, c] = both
            xs[t, c] = both.astype(BF16)

            def spread_out(n, _):
                remote(
                    xs.at[t, c, lax.rem(chip + n, 8)],
                    xr.at[t, c, n - 1],
                    xss.at[2 * t + c],
                    xrs.at[2 * t + c],
                    tp=chip_at(n),
                ).start()
                return 0

            lax.fori_loop(1, 8, spread_out, 0)
            left_of(xr.at[t, c], xss.at[2 * t + c])
    for c in range(NCH):
        totals = []
        for t in range(2):
            local(xr.at[t, c], xr.at[t, c], xrs.at[2 * t + c]).wait()
            total = sums[t, c, chip]
            for n in range(7):
                total = total + xr[t, c, n].astype(F32)
            totals.append(total)
        for half in range(2):
            for r in range(6):
                at = 8 * half + r
                out[r, :, pl.ds(CH * c + CH // 2 * half, CH // 2)] = jnp.concatenate(
                    [total[at : at + 1] for total in totals], axis=0
                ).astype(BF16)

    for wait in left:
        wait()


def shards(
    queries,
    row_prompt,
    owner_slot,
    suffix_len,
    prefix_keys,
    prefix_values,
    suffix_keys,
    suffix_values,
    new_keys,
    new_values,
    out_weight,
):
    smem = pl.BlockSpec(memory_space=pltpu.SMEM)
    vmem = pl.BlockSpec(memory_space=pltpu.VMEM)
    hbm = pl.BlockSpec(memory_space=pl.ANY)
    sem = pltpu.SemaphoreType.DMA
    scratch = [
        pltpu.VMEM((2, HALVES, 128, HD), BF16),
        pltpu.VMEM((OWN, KEYS, HD), BF16),
        pltpu.VMEM((OWN, KEYS, 2 * HD), BF16),
        pltpu.VMEM((HALVES, 384, HD), BF16),
        pltpu.VMEM((HALVES, 384, HD), BF16),
        pltpu.VMEM((512, D), BF16),
        pltpu.VMEM((NI, 1, HD), I32),
        pltpu.VMEM((1, HD), I32),
        pltpu.SMEM((1, HD), I32),
        pltpu.VMEM((BLOCKS, 16, HD), BF16),
        pltpu.VMEM((NI, OWN, 16, HD), BF16),
        pltpu.VMEM((2, 2, 8, OWN, 16, HD), BF16),
        pltpu.VMEM((2, 2, 8, OWN, 16, HD), BF16),
        pltpu.VMEM((SLOTS, 16, HD), BF16),
        pltpu.VMEM((BLOCKS, 16, HD), BF16),
        pltpu.VMEM((2, 8, HALVES, 16, HD), BF16),
        pltpu.VMEM((NI * 8, 1, HD), F32),
        pltpu.VMEM((HALVES, 256, HD), F32),
        pltpu.VMEM((HALVES, 256, HD), F32),
        pltpu.VMEM((HALVES, 256, HD), F32),
        pltpu.VMEM((2, 400, HD), F32),
        pltpu.VMEM((2, 128, 512), BF16),
        pltpu.VMEM((2, NCH, 64, CH), F32),
        pltpu.VMEM((2, NCH, 64, CH), BF16),
        pltpu.VMEM((2, NCH, 64, CH), BF16),
        pltpu.VMEM((2, NCH, 8, 16, CH // 2), BF16),
        pltpu.VMEM((2, NCH, 7, 16, CH // 2), BF16),
        pltpu.VMEM((2, NCH, 8, 16, CH // 2), F32),
        sem((17,)),
        sem((8,)),
        sem((8,)),
        sem((2 * NCH,)),
        sem((2 * NCH,)),
        sem((2 * NCH,)),
        sem((2 * NCH,)),
    ]
    return pl.pallas_call(
        kernel,
        out_shape=jax.ShapeDtypeStruct((6, 2, D), BF16),
        in_specs=[smem, smem, vmem] + [hbm] * 8,
        out_specs=vmem,
        scratch_shapes=scratch,
        compiler_params=pltpu.CompilerParams(
            collective_id=0, has_side_effects=True, vmem_limit_bytes=56 * 1024 * 1024
        ),
    )(
        row_prompt,
        owner_slot,
        suffix_len.reshape(1, 96),
        queries.reshape(2, 384, HD),
        prefix_keys.reshape(OWN, KEYS, HD),
        prefix_values.reshape(OWN, KEYS, HD),
        suffix_keys.reshape(768, HD),
        suffix_values.reshape(768, HD),
        new_keys.reshape(2, 96, HD),
        new_values.reshape(2, 96, HD),
        out_weight,
    )


def solution(mesh):
    placed = (
        P(None, "inst", "tp", None),
        P("inst"),
        P(),
        P("inst"),
        P("inst", None, "tp", None),
        P("inst", None, "tp", None),
        P("inst", None, "tp", None),
        P("inst", None, "tp", None),
        P(None, "inst", "tp", None),
        P(None, "inst", "tp", None),
        P("tp", None),
    )
    return jax.shard_map(
        shards, mesh=mesh, in_specs=placed, out_specs=P(("inst", "tp"), None, None), check_vma=False
    )
```

```python
import math

import jax
import jax.numpy as jnp
from jax import lax
from jax.experimental import pallas as pl
from jax.experimental.pallas import tpu as pltpu
from jax.sharding import PartitionSpec as P

F32 = jnp.float32
BF16 = jnp.bfloat16
I32 = jnp.int32

NI = 32
NZ = 16
HALVES = 3
BLOCKS = 48
SLOTS = 64
OWN = 2
HD = 128
KEYS = 4096
D = 2560
CH = 1280
NCH = D // CH
KC = 1024
U_OF = (0, 2, 1)
SCALE = 1.0 / math.sqrt(HD)
C2 = SCALE * math.log2(math.e)
NEG = -1e30


def dot_t(a, b):
    return lax.dot_general(a, b, (((1,), (1,)), ((), ())), preferred_element_type=F32)


def dot(a, b):
    return lax.dot_general(a, b, (((1,), (0,)), ((), ())), preferred_element_type=F32)


def iota(shape, dim):
    return lax.broadcasted_iota(I32, shape, dim)


def far_first(k, n):
    up = lax.rem(k + 1, 2)
    return lax.rem(n // 2 + up * lax.div(k, 2) + (1 - up) * (n - lax.div(k + 1, 2)), n)


def kernel(
    row_prompt,
    owner_slot,
    lens,
    q_hbm,
    k_hbm,
    v_hbm,
    sk_hbm,
    sv_hbm,
    nk_hbm,
    nv_hbm,
    w_hbm,
    out,
    q,
    kk,
    va,
    ck,
    cv,
    w,
    tab,
    inv_v,
    inv_s,
    mid,
    snd,
    qin,
    obuf,
    mid2,
    snd2,
    pin,
    tvec,
    tmid,
    tsnd,
    spare,
    tin,
    own_acc,
    own_m,
    own_l,
    att,
    lhs,
    mine,
    cs,
    cr,
    xs,
    xr,
    sums,
    ld,
    ss,
    rs,
    css,
    crs,
    xss,
    xrs,
):
    inst = lax.axis_index("inst")
    tp = lax.axis_index("tp")
    yy = lax.div(inst, NZ)
    zz = lax.rem(inst, NZ)
    core = lax.rem(tp, 2)
    chip = lax.div(tp, 2)
    partner = tp + 1 - 2 * core
    my_t = lax.rem(zz, 2)
    my_m = lax.div(zz, 2)

    def remote(src, dst, s, r, **where):
        return pltpu.make_async_remote_copy(
            src_ref=src, dst_ref=dst, send_sem=s, recv_sem=r,
            device_id=where, device_id_type=pl.DeviceIdType.MESH,
        )

    def local(src, dst, s):
        return pltpu.make_async_copy(src, dst, s)

    def chip_at(step):
        return lax.rem(chip + step, 8) * 2 + core

    left = []

    def left_of(ref, sem):
        left.append(lambda: local(ref, ref, sem).wait())

    loads_q = [
        local(q_hbm.at[:, pl.ds(128 * U_OF[o], 128)], q.at[:, o], ld.at[0]) for o in range(HALVES)
    ]
    for c in loads_q:
        c.start()
    loads_own = []
    for o in range(HALVES):
        u = U_OF[o]
        for src, dst, sem in ((sk_hbm, ck, 3), (sv_hbm, cv, 4)):
            loads_own.append(
                local(src.at[pl.ds(256 * u, 256)], dst.at[o, pl.ds(0, 256)], ld.at[sem + 4 * o])
            )
        for src, dst, sem in ((nk_hbm, ck, 5), (nv_hbm, cv, 6)):
            loads_own.append(
                local(
                    src.at[:, pl.ds(32 * u, 32)],
                    dst.at[o, pl.ds(256, 64)].reshape(2, 32, HD),
                    ld.at[sem + 4 * o],
                )
            )
    for c in loads_own:
        c.start()
    load_k = local(k_hbm, kk, ld.at[1])
    load_k.start()
    load_v = local(v_hbm, va.at[:, :, pl.ds(0, HD)], ld.at[2])
    load_v.start()
    load_w = local(w_hbm, w, ld.at[15])
    load_w.start()

    barrier = pltpu.get_barrier_semaphore()

    def greet(k, _):
        z = lax.rem(zz + far_first(k, NZ), NZ)
        for y in (1 - yy, yy):
            pl.semaphore_signal(
                barrier, inc=1, device_id={"inst": y * NZ + z},
                device_id_type=pl.DeviceIdType.MESH,
            )
        return 0

    lax.fori_loop(0, NZ - 1, greet, 0)
    pl.semaphore_signal(
        barrier, inc=1, device_id={"inst": (1 - yy) * NZ + zz}, device_id_type=pl.DeviceIdType.MESH
    )

    def greet_chip(n, _):
        pl.semaphore_signal(
            barrier, inc=1, device_id={"tp": chip_at(n)}, device_id_type=pl.DeviceIdType.MESH
        )
        return 0

    lax.fori_loop(1, 8, greet_chip, 0)
    pl.semaphore_signal(
        barrier, inc=1, device_id={"tp": partner}, device_id_type=pl.DeviceIdType.MESH
    )

    lane1 = iota((1, HD), 1)
    head = jnp.zeros((1, HD), I32)
    for u in range(HALVES):
        block = lax.div(HALVES * inst + u, 2)
        first = lax.rem(HALVES * inst + u, 2) == 0
        slot = owner_slot[row_prompt[32 * u]]
        head += jnp.where((lane1 == slot) & first, block, 0)
        head += jnp.where((lane1 == SLOTS + block) & first, slot, 0)
    tab[inst] = head
    ones = jnp.ones((256, HD), BF16)

    def set_ones(n, _):
        va[lax.div(n, 16), pl.ds(pl.multiple_of(lax.rem(n, 16) * 256, 256), 256), pl.ds(HD, HD)] = ones
        return 0

    lax.fori_loop(0, 32, set_ones, 0)
    for o in range(HALVES):
        ck[o, pl.ds(320, 64)] = jnp.zeros((64, HD), BF16)
        cv[o, pl.ds(320, 64)] = jnp.zeros((64, HD), BF16)
    for c in loads_q:
        c.wait()

    pl.semaphore_wait(barrier, NI - 1 + 1 + 7)

    b_outer = lax.div(HALVES * inst, 2)
    b_inner = lax.div(HALVES * inst + 1, 2)
    side_outer = lax.rem(zz, 2)
    side_inner = 1 - side_outer

    def outer_piece(z):
        at = pl.ds(pl.multiple_of(16 * lax.div(z, 2), 16), 16)
        return q.at[lax.rem(z, 2), pl.ds(0, 2), at], mid.at[pl.ds(b_outer, 2)]

    def inner_piece(z):
        at = pl.ds(pl.multiple_of(16 * lax.div(z, 2), 16), 16)
        return q.at[lax.rem(z, 2), 2, at], mid.at[b_inner]

    def send_head(d):
        remote(tab.at[inst], tab.at[inst], ss.at[0], rs.at[0], inst=d).start()

    def send_pieces(z):
        send_head(side_outer * NZ + z)
        send_head(side_inner * NZ + z)
        remote(*outer_piece(z), ss.at[1], rs.at[1], inst=side_outer * NZ + z).start()
        remote(*inner_piece(z), ss.at[1], rs.at[1], inst=side_inner * NZ + z).start()

    bases = [lax.rem(zz + lax.rem(zz + t, 2), NZ) for t in range(2)]
    across = (1 - yy) * NZ + zz
    for t in range(2):

        def send_step(k, _):
            send_pieces(lax.rem(bases[t] + 2 * far_first(k, 8), NZ))
            return 0

        lax.fori_loop(0, 7, send_step, 0)

        @pl.when(my_t != t)
        def _():
            send_pieces(bases[t])

        @pl.when((my_t == t) & (side_outer == yy))
        def _():
            send_head(across)
            local(*outer_piece(zz), rs.at[1]).start()
            remote(*inner_piece(zz), ss.at[1], rs.at[1], inst=across).start()

        @pl.when((my_t == t) & (side_outer != yy))
        def _():
            send_head(across)
            local(*inner_piece(zz), rs.at[1]).start()
            remote(*outer_piece(zz), ss.at[1], rs.at[1], inst=across).start()

    heads_all = tab.at[pl.ds(0, NI - 1)]
    left_of(heads_all, ss.at[0])
    kept_here = 1 + jnp.where(side_outer == yy, 1, 0)

    def left_halves(ref, sem):
        def wait():
            for n_kept in (1, 2):

                @pl.when(kept_here == n_kept)
                def _():
                    sent = ref.at[pl.ds(0, BLOCKS - n_kept)]
                    local(sent, sent, sem).wait()

        left.append(wait)

    left_halves(mid, ss.at[1])

    for c in loads_own:
        c.wait()
    lens_b = jnp.broadcast_to(lens[...].astype(F32), (8, 96)).astype(BF16)
    for o in range(HALVES):
        u = U_OF[o]
        at96 = iota((96, 384), 0)
        lane96 = iota((96, 384), 1)
        spread = jnp.where(at96 == 32 * u + lax.div(lane96, 8), 1.0, 0.0).astype(BF16)
        len_row = dot(lens_b, spread)[0:1]
        row = iota((256, 384), 0)
        lane = iota((256, 384), 1)
        sample = lax.div(lax.rem(row, 128), 4)
        step = lax.div(row, 128)
        cached = (lane < 256) & (lax.div(lane, 8) == sample) & (
            lax.rem(lane, 8).astype(F32) < jnp.broadcast_to(len_row, (256, 384))
        )
        new_at = lane - 256
        new = (lane >= 256) & (lane < 320) & (lax.rem(new_at, 32) == sample) & (
            lax.div(new_at, 32) <= step
        )
        qu = jnp.concatenate([q[0, o], q[1, o]], axis=0)
        s = jnp.where(cached | new, dot_t(qu, ck[o]), NEG)
        top = jnp.max(s, axis=1, keepdims=True)
        p = jnp.exp2(s * C2 - top * C2)
        own_m[o] = jnp.broadcast_to(top * SCALE, (256, HD))
        own_l[o] = jnp.broadcast_to(jnp.sum(p, axis=1, keepdims=True), (256, HD))
        own_acc[o] = dot(p.astype(BF16), cv[o])

    local(heads_all, heads_all, rs.at[0]).wait()
    inv_v[...] = jnp.sum(tab[...], axis=0)
    to_smem = local(inv_v, inv_s, ld.at[16])
    to_smem.start()
    to_smem.wait()

    def slot_block(s):
        return jnp.clip(inv_s[0, s], 0, BLOCKS - 1)

    def block_slot(n):
        return jnp.clip(inv_s[0, SLOTS + n], 0, SLOTS - 1)

    local(mid, mid, rs.at[1]).wait()

    def select(d):
        for e in range(OWN):
            snd[d, e] = mid[slot_block(OWN * d + e)]

    def to_owner(d):
        return remote(snd.at[d], qin.at[my_t, yy, my_m], ss.at[2], rs.at[2 + my_t], inst=d)

    def send_selected(k, _):
        z = lax.rem(zz + far_first(k, NZ), NZ)
        for y in (1 - yy, yy):
            d = y * NZ + z
            select(d)
            to_owner(d).start()
        return 0

    lax.fori_loop(0, NZ - 1, send_selected, 0)
    select(across)
    to_owner(across).start()
    select(inst)
    local(snd.at[inst], qin.at[my_t, yy, my_m], rs.at[2 + my_t]).start()
    left_of(snd.at[pl.ds(0, NI - 1)], ss.at[2])

    load_k.wait()
    load_v.wait()
    eye = iota((HD, HD), 0) == iota((HD, HD), 1)
    for t in range(2):
        local(qin.at[t], qin.at[t], rs.at[2 + t]).wait()
        for e in range(OWN):
            qv = qin[t, :, :, e].reshape(256, HD)
            top = jnp.full((256, 1), NEG, F32)
            acc = jnp.zeros((256, 2 * HD), F32)
            for c in range(KEYS // KC):
                s = dot_t(qv, kk[e, pl.ds(KC * c, KC)])
                part = s[:, :HD]
                for j in range(1, KC // HD):
                    part = jnp.maximum(part, s[:, HD * j : HD * (j + 1)])
                higher = jnp.maximum(top, jnp.max(part, axis=1, keepdims=True))
                p = jnp.exp2(s * C2 - higher * C2)
                again = jnp.exp2((top - higher) * C2)
                acc = acc * again + dot(p.astype(BF16), va[e, pl.ds(KC * c, KC)])
                top = higher
            weight = acc[:, HD:]
            obuf[t, :, :, e] = (acc[:, :HD] / weight).astype(BF16).reshape(2, 8, 16, HD)
            total = top * SCALE + jnp.log(weight)
            for y in range(2):
                tvec[t, y, e] = jnp.sum(
                    jnp.where(eye, total[HD * y : HD * (y + 1)], 0.0), axis=0, keepdims=True
                )
        base = bases[t]
        slots = mid2.at[pl.ds(OWN * inst, OWN)]
        slots_t = tmid.at[pl.ds(OWN * inst, OWN)]

        def back_to(y, z):
            d = y * NZ + z
            remote(obuf.at[t, y, lax.div(z, 2)], slots, ss.at[4], rs.at[4], inst=d).start()
            remote(tvec.at[t, y], slots_t, ss.at[5], rs.at[5], inst=d).start()

        def back(k, _):
            z = lax.rem(base + 2 * far_first(k, 8), NZ)
            for y in (1 - yy, yy):
                back_to(y, z)
            return 0

        lax.fori_loop(0, 7, back, 0)
        back_to(1 - yy, base)

        @pl.when(my_t == t)
        def _():
            local(obuf.at[t, yy, my_m], slots, rs.at[4]).start()
            local(tvec.at[t, yy], slots_t, rs.at[5]).start()

        @pl.when(my_t != t)
        def _():
            back_to(yy, base)

    left_of(mid2.at[pl.ds(0, OWN * (NI - 1))], ss.at[4])

    left_of(tmid.at[pl.ds(0, OWN * (NI - 1))], ss.at[5])

    local(mid2, mid2, rs.at[4]).wait()
    local(tmid, tmid, rs.at[5]).wait()

    def select2(n, _):
        snd2[n] = mid2[block_slot(n)]
        return 0

    lax.fori_loop(0, BLOCKS, select2, 0)

    def home(d, kept):
        outer = snd2.at[pl.ds(lax.div(HALVES * d, 2), 2)], pin.at[my_t, my_m, pl.ds(0, 2)]
        inner = snd2.at[lax.div(HALVES * d + 1, 2)], pin.at[my_t, my_m, 2]
        for refs, parity in ((outer, 0), (inner, 1)):

            @pl.when(lax.rem(d + yy, 2) == parity)
            def _():
                if kept:
                    local(*refs, rs.at[6 + my_t]).start()
                else:
                    remote(*refs, ss.at[6], rs.at[6 + my_t], inst=d).start()

    def send_home(k, _):
        z = lax.rem(zz + far_first(k, NZ), NZ)
        for y in (1 - yy, yy):
            home(y * NZ + z, False)
        return 0

    lax.fori_loop(0, NZ - 1, send_home, 0)
    home(across, False)
    home(inst, True)
    left_halves(snd2, ss.at[6])

    def total_home(i, _):
        n = my_m + 8 * i
        tsnd[i] = tmid[block_slot(n)]
        d = lax.div(2 * n + yy, HALVES)
        to = tin.at[my_t, lax.rem(2 * lax.rem(2 * n + yy, HALVES), HALVES)]

        @pl.when(d == inst)
        def _():
            local(tsnd.at[i], to, rs.at[8 + my_t]).start()
            local(tsnd.at[i], spare.at[i], ss.at[7]).start()

        @pl.when(d != inst)
        def _():
            remote(tsnd.at[i], to, ss.at[7], rs.at[8 + my_t], inst=d).start()

        return 0

    lax.fori_loop(0, BLOCKS // 8, total_home, 0)
    left_of(tsnd, ss.at[7])

    load_w.wait()
    for t in range(2):
        local(pin.at[t], pin.at[t], rs.at[6 + t]).wait()
        local(tin.at[t], tin.at[t], rs.at[8 + t]).wait()
        for o in range(HALVES):
            total = jnp.sum(
                jnp.where(eye, jnp.broadcast_to(tin[t, o], (HD, HD)), 0.0), axis=1, keepdims=True
            )
            rows = pl.ds(HD * t, HD)
            own_top = own_m[o, rows]
            top = jnp.maximum(total, own_top)
            carried = jnp.exp(total - top)
            own = jnp.exp(own_top - top)
            below = carried + own * own_l[o, rows]
            before = pin[t, :, o].reshape(HD, HD).astype(F32)
            att[t, pl.ds(HD * U_OF[o], HD)] = (carried * before + own * own_acc[o, rows]) / below
        att[t, pl.ds(384, 16)] = jnp.zeros((16, HD), F32)
        for c in range(2):
            for a in range(0, 8, 2):
                for h in range(4):
                    pair = [att[t, pl.ds(24 * (2 * b + c) + h, 8, stride=4)] for b in (a, a + 1)]
                    lhs[t, pl.ds(64 * c + 8 * a, 16), pl.ds(HD * h, HD)] = jnp.concatenate(
                        pair, axis=0
                    ).astype(BF16)
        for c in range(NCH):
            part = dot(lhs[t], w[:, pl.ds(CH * c, CH)])
            cs[t, c] = jnp.where(core == 0, part[64:], part[:64]).astype(BF16)
            mine[t, c] = jnp.where(core == 0, part[:64], part[64:])
            remote(
                cs.at[t, c], cr.at[t, c], css.at[2 * t + c], crs.at[2 * t + c], tp=partner
            ).start()
        for c in range(NCH):
            pair_copy = remote(
                cs.at[t, c], cr.at[t, c], css.at[2 * t + c], crs.at[2 * t + c], tp=partner
            )
            pair_copy.wait_recv()
            left.append(pair_copy.wait_send)
            both = (mine[t, c] + cr[t, c].astype(F32)).reshape(8, 8, CH)
            both = jnp.concatenate([both[:, :, : CH // 2], both[:, :, CH // 2 :]], axis=1)
            sums[t, c] = both
            xs[t, c] = both.astype(BF16)

            def spread_out(n, _):
                remote(
                    xs.at[t, c, lax.rem(chip + n, 8)],
                    xr.at[t, c, n - 1],
                    xss.at[2 * t + c],
                    xrs.at[2 * t + c],
                    tp=chip_at(n),
                ).start()
                return 0

            lax.fori_loop(1, 8, spread_out, 0)
            left_of(xr.at[t, c], xss.at[2 * t + c])
    for c in range(NCH):
        totals = []
        for t in range(2):
            local(xr.at[t, c], xr.at[t, c], xrs.at[2 * t + c]).wait()
            total = sums[t, c, chip]
            for n in range(7):
                total = total + xr[t, c, n].astype(F32)
            totals.append(total)
        for half in range(2):
            for r in range(6):
                at = 8 * half + r
                out[r, :, pl.ds(CH * c + CH // 2 * half, CH // 2)] = jnp.concatenate(
                    [total[at : at + 1] for total in totals], axis=0
                ).astype(BF16)

    for wait in left:
        wait()


def shards(
    queries,
    row_prompt,
    owner_slot,
    suffix_len,
    prefix_keys,
    prefix_values,
    suffix_keys,
    suffix_values,
    new_keys,
    new_values,
    out_weight,
):
    smem = pl.BlockSpec(memory_space=pltpu.SMEM)
    vmem = pl.BlockSpec(memory_space=pltpu.VMEM)
    hbm = pl.BlockSpec(memory_space=pl.ANY)
    sem = pltpu.SemaphoreType.DMA
    scratch = [
        pltpu.VMEM((2, HALVES, 128, HD), BF16),
        pltpu.VMEM((OWN, KEYS, HD), BF16),
        pltpu.VMEM((OWN, KEYS, 2 * HD), BF16),
        pltpu.VMEM((HALVES, 384, HD), BF16),
        pltpu.VMEM((HALVES, 384, HD), BF16),
        pltpu.VMEM((512, D), BF16),
        pltpu.VMEM((NI, 1, HD), I32),
        pltpu.VMEM((1, HD), I32),
        pltpu.SMEM((1, HD), I32),
        pltpu.VMEM((BLOCKS, 16, HD), BF16),
        pltpu.VMEM((NI, OWN, 16, HD), BF16),
        pltpu.VMEM((2, 2, 8, OWN, 16, HD), BF16),
        pltpu.VMEM((2, 2, 8, OWN, 16, HD), BF16),
        pltpu.VMEM((SLOTS, 16, HD), BF16),
        pltpu.VMEM((BLOCKS, 16, HD), BF16),
        pltpu.VMEM((2, 8, HALVES, 16, HD), BF16),
        pltpu.VMEM((2, 2, OWN, 1, HD), F32),
        pltpu.VMEM((SLOTS, 1, HD), F32),
        pltpu.VMEM((BLOCKS // 8, 1, HD), F32),
        pltpu.VMEM((BLOCKS // 8, 1, HD), F32),
        pltpu.VMEM((2, HALVES, 1, HD), F32),
        pltpu.VMEM((HALVES, 256, HD), F32),
        pltpu.VMEM((HALVES, 256, HD), F32),
        pltpu.VMEM((HALVES, 256, HD), F32),
        pltpu.VMEM((2, 400, HD), F32),
        pltpu.VMEM((2, 128, 512), BF16),
        pltpu.VMEM((2, NCH, 64, CH), F32),
        pltpu.VMEM((2, NCH, 64, CH), BF16),
        pltpu.VMEM((2, NCH, 64, CH), BF16),
        pltpu.VMEM((2, NCH, 8, 16, CH // 2), BF16),
        pltpu.VMEM((2, NCH, 7, 16, CH // 2), BF16),
        pltpu.VMEM((2, NCH, 8, 16, CH // 2), F32),
        sem((17,)),
        sem((8,)),
        sem((10,)),
        sem((2 * NCH,)),
        sem((2 * NCH,)),
        sem((2 * NCH,)),
        sem((2 * NCH,)),
    ]
    return pl.pallas_call(
        kernel,
        out_shape=jax.ShapeDtypeStruct((6, 2, D), BF16),
        in_specs=[smem, smem, vmem] + [hbm] * 8,
        out_specs=vmem,
        scratch_shapes=scratch,
        compiler_params=pltpu.CompilerParams(
            collective_id=0, has_side_effects=True, vmem_limit_bytes=56 * 1024 * 1024
        ),
    )(
        row_prompt,
        owner_slot,
        suffix_len.reshape(1, 96),
        queries.reshape(2, 384, HD),
        prefix_keys.reshape(OWN, KEYS, HD),
        prefix_values.reshape(OWN, KEYS, HD),
        suffix_keys.reshape(768, HD),
        suffix_values.reshape(768, HD),
        new_keys.reshape(2, 96, HD),
        new_values.reshape(2, 96, HD),
        out_weight,
    )


def solution(mesh):
    placed = (
        P(None, "inst", "tp", None),
        P("inst"),
        P(),
        P("inst"),
        P("inst", None, "tp", None),
        P("inst", None, "tp", None),
        P("inst", None, "tp", None),
        P("inst", None, "tp", None),
        P(None, "inst", "tp", None),
        P(None, "inst", "tp", None),
        P("tp", None),
    )
    return jax.shard_map(
        shards, mesh=mesh, in_specs=placed, out_specs=P(("inst", "tp"), None, None), check_vma=False
    )
```

```python
import math

import jax
import jax.numpy as jnp
from jax import lax
from jax.experimental import pallas as pl
from jax.experimental.pallas import tpu as pltpu
from jax.sharding import PartitionSpec as P

F32 = jnp.float32
BF16 = jnp.bfloat16
I32 = jnp.int32

NI = 32
NZ = 16
HALVES = 3
BLOCKS = 48
SLOTS = 64
EARLY = 4
OWN = 2
HD = 128
KEYS = 4096
D = 2560
CH = 1280
NCH = D // CH
KC = 1024
U_OF = (0, 2, 1)
SCALE = 1.0 / math.sqrt(HD)
C2 = SCALE * math.log2(math.e)
NEG = -1e30


def dot_t(a, b):
    return lax.dot_general(a, b, (((1,), (1,)), ((), ())), preferred_element_type=F32)


def dot(a, b):
    return lax.dot_general(a, b, (((1,), (0,)), ((), ())), preferred_element_type=F32)


def iota(shape, dim):
    return lax.broadcasted_iota(I32, shape, dim)


def far_first(k, n):
    up = lax.rem(k + 1, 2)
    return lax.rem(n // 2 + up * lax.div(k, 2) + (1 - up) * (n - lax.div(k + 1, 2)), n)


def kernel(
    row_prompt,
    owner_slot,
    lens,
    q_hbm,
    k_hbm,
    v_hbm,
    sk_hbm,
    sv_hbm,
    nk_hbm,
    nv_hbm,
    w_hbm,
    out,
    q,
    kk,
    va,
    ck,
    cv,
    w,
    tab,
    inv_v,
    inv_s,
    mid,
    snd,
    qin,
    obuf,
    mid2,
    snd2,
    pin,
    tvec,
    tmid,
    tsnd,
    spare,
    tin,
    own_acc,
    own_m,
    own_l,
    att,
    lhs,
    mine,
    cs,
    cr,
    xs,
    xr,
    sums,
    step0,
    ld,
    ss,
    rs,
    css,
    crs,
    xss,
    xrs,
):
    inst = lax.axis_index("inst")
    tp = lax.axis_index("tp")
    yy = lax.div(inst, NZ)
    zz = lax.rem(inst, NZ)
    core = lax.rem(tp, 2)
    chip = lax.div(tp, 2)
    partner = tp + 1 - 2 * core
    my_t = lax.rem(zz, 2)
    my_m = lax.div(zz, 2)
    has_totals = lax.rem(zz, 8) < 2

    def remote(src, dst, s, r, **where):
        return pltpu.make_async_remote_copy(
            src_ref=src, dst_ref=dst, send_sem=s, recv_sem=r,
            device_id=where, device_id_type=pl.DeviceIdType.MESH,
        )

    def local(src, dst, s):
        return pltpu.make_async_copy(src, dst, s)

    def chip_at(step):
        return lax.rem(chip + step, 8) * 2 + core

    left = []

    def left_of(ref, sem):
        left.append(lambda: local(ref, ref, sem).wait())

    loads_q = [
        local(q_hbm.at[:, pl.ds(128 * U_OF[o], 128)], q.at[:, o], ld.at[0]) for o in range(HALVES)
    ]
    for c in loads_q:
        c.start()
    loads_own = []
    for o in range(HALVES):
        u = U_OF[o]
        for src, dst, sem in ((sk_hbm, ck, 3), (sv_hbm, cv, 4)):
            loads_own.append(
                local(src.at[pl.ds(256 * u, 256)], dst.at[o, pl.ds(0, 256)], ld.at[sem + 4 * o])
            )
        for src, dst, sem in ((nk_hbm, ck, 5), (nv_hbm, cv, 6)):
            loads_own.append(
                local(
                    src.at[:, pl.ds(32 * u, 32)],
                    dst.at[o, pl.ds(256, 64)].reshape(2, 32, HD),
                    ld.at[sem + 4 * o],
                )
            )
    for c in loads_own:
        c.start()
    load_k = local(k_hbm, kk, ld.at[1])
    load_k.start()
    load_v = local(v_hbm, va.at[:, :, pl.ds(0, HD)], ld.at[2])
    load_v.start()
    load_w = local(w_hbm, w, ld.at[15])
    load_w.start()

    barrier = pltpu.get_barrier_semaphore()

    def greet(k, _):
        z = lax.rem(zz + far_first(k, NZ), NZ)
        for y in (1 - yy, yy):
            pl.semaphore_signal(
                barrier, inc=1, device_id={"inst": y * NZ + z},
                device_id_type=pl.DeviceIdType.MESH,
            )
        return 0

    lax.fori_loop(0, NZ - 1, greet, 0)
    pl.semaphore_signal(
        barrier, inc=1, device_id={"inst": (1 - yy) * NZ + zz}, device_id_type=pl.DeviceIdType.MESH
    )

    def greet_chip(n, _):
        pl.semaphore_signal(
            barrier, inc=1, device_id={"tp": chip_at(n)}, device_id_type=pl.DeviceIdType.MESH
        )
        return 0

    lax.fori_loop(1, 8, greet_chip, 0)
    pl.semaphore_signal(
        barrier, inc=1, device_id={"tp": partner}, device_id_type=pl.DeviceIdType.MESH
    )

    lane1 = iota((1, HD), 1)
    head = jnp.zeros((1, HD), I32)
    for u in range(HALVES):
        block = lax.div(HALVES * inst + u, 2)
        first = lax.rem(HALVES * inst + u, 2) == 0
        slot = owner_slot[row_prompt[32 * u]]
        head += jnp.where((lane1 == slot) & first, block, 0)
        head += jnp.where((lane1 == SLOTS + block) & first, slot, 0)
    tab[inst] = head
    ones = jnp.ones((256, HD), BF16)

    def set_ones(n, _):
        va[lax.div(n, 16), pl.ds(pl.multiple_of(lax.rem(n, 16) * 256, 256), 256), pl.ds(HD, HD)] = ones
        return 0

    lax.fori_loop(0, 32, set_ones, 0)
    for o in range(HALVES):
        ck[o, pl.ds(320, 64)] = jnp.zeros((64, HD), BF16)
        cv[o, pl.ds(320, 64)] = jnp.zeros((64, HD), BF16)
    for c in loads_q:
        c.wait()

    pl.semaphore_wait(barrier, NI - 1 + 1 + 7)

    b_outer = lax.div(HALVES * inst, 2)
    b_inner = lax.div(HALVES * inst + 1, 2)
    side_outer = lax.rem(zz, 2)
    side_inner = 1 - side_outer

    def outer_piece(z):
        at = pl.ds(pl.multiple_of(16 * lax.div(z, 2), 16), 16)
        return q.at[lax.rem(z, 2), pl.ds(0, 2), at], mid.at[pl.ds(b_outer, 2)]

    def inner_piece(z):
        at = pl.ds(pl.multiple_of(16 * lax.div(z, 2), 16), 16)
        return q.at[lax.rem(z, 2), 2, at], mid.at[b_inner]

    def send_head(d):
        remote(tab.at[inst], tab.at[inst], ss.at[0], rs.at[0], inst=d).start()

    def send_pieces(z):
        send_head(side_outer * NZ + z)
        send_head(side_inner * NZ + z)
        remote(*outer_piece(z), ss.at[1], rs.at[1], inst=side_outer * NZ + z).start()
        remote(*inner_piece(z), ss.at[1], rs.at[1], inst=side_inner * NZ + z).start()

    bases = [lax.rem(zz + lax.rem(zz + t, 2), NZ) for t in range(2)]
    across = (1 - yy) * NZ + zz
    for t in range(2):

        def send_step(k, _):
            send_pieces(lax.rem(bases[t] + 2 * far_first(k, 8), NZ))
            return 0

        lax.fori_loop(0, 7, send_step, 0)

        @pl.when(my_t != t)
        def _():
            send_pieces(bases[t])

        @pl.when((my_t == t) & (side_outer == yy))
        def _():
            send_head(across)
            local(*outer_piece(zz), rs.at[1]).start()
            remote(*inner_piece(zz), ss.at[1], rs.at[1], inst=across).start()

        @pl.when((my_t == t) & (side_outer != yy))
        def _():
            send_head(across)
            local(*inner_piece(zz), rs.at[1]).start()
            remote(*outer_piece(zz), ss.at[1], rs.at[1], inst=across).start()

    heads_all = tab.at[pl.ds(0, NI - 1)]
    left_of(heads_all, ss.at[0])
    kept_here = 1 + jnp.where(side_outer == yy, 1, 0)

    def left_halves(ref, sem):
        def wait():
            for n_kept in (1, 2):

                @pl.when(kept_here == n_kept)
                def _():
                    sent = ref.at[pl.ds(0, BLOCKS - n_kept)]
                    local(sent, sent, sem).wait()

        left.append(wait)

    left_halves(mid, ss.at[1])

    for c in loads_own:
        c.wait()
    lens_b = jnp.broadcast_to(lens[...].astype(F32), (8, 96)).astype(BF16)
    for o in range(HALVES):
        u = U_OF[o]
        at96 = iota((96, 384), 0)
        lane96 = iota((96, 384), 1)
        spread = jnp.where(at96 == 32 * u + lax.div(lane96, 8), 1.0, 0.0).astype(BF16)
        len_row = dot(lens_b, spread)[0:1]
        row = iota((256, 384), 0)
        lane = iota((256, 384), 1)
        sample = lax.div(lax.rem(row, 128), 4)
        step = lax.div(row, 128)
        cached = (lane < 256) & (lax.div(lane, 8) == sample) & (
            lax.rem(lane, 8).astype(F32) < jnp.broadcast_to(len_row, (256, 384))
        )
        new_at = lane - 256
        new = (lane >= 256) & (lane < 320) & (lax.rem(new_at, 32) == sample) & (
            lax.div(new_at, 32) <= step
        )
        qu = jnp.concatenate([q[0, o], q[1, o]], axis=0)
        s = jnp.where(cached | new, dot_t(qu, ck[o]), NEG)
        top = jnp.max(s, axis=1, keepdims=True)
        p = jnp.exp2(s * C2 - top * C2)
        own_m[o] = jnp.broadcast_to(top * SCALE, (256, HD))
        own_l[o] = jnp.broadcast_to(jnp.sum(p, axis=1, keepdims=True), (256, HD))
        own_acc[o] = dot(p.astype(BF16), cv[o])

    local(heads_all, heads_all, rs.at[0]).wait()
    inv_v[...] = jnp.sum(tab[...], axis=0)
    to_smem = local(inv_v, inv_s, ld.at[16])
    to_smem.start()
    to_smem.wait()

    def slot_block(s):
        return jnp.clip(inv_s[0, s], 0, BLOCKS - 1)

    def block_slot(n):
        return jnp.clip(inv_s[0, SLOTS + n], 0, SLOTS - 1)

    local(mid, mid, rs.at[1]).wait()

    def select(d):
        for e in range(OWN):
            snd[d, e] = mid[slot_block(OWN * d + e)]

    def to_owner(d):
        return remote(snd.at[d], qin.at[my_t, yy, my_m], ss.at[2], rs.at[2 + my_t], inst=d)

    def send_selected(k, _):
        z = lax.rem(zz + far_first(k, NZ), NZ)
        for y in (1 - yy, yy):
            d = y * NZ + z
            select(d)
            to_owner(d).start()
        return 0

    lax.fori_loop(0, NZ - 1, send_selected, 0)
    select(across)
    to_owner(across).start()
    select(inst)
    local(snd.at[inst], qin.at[my_t, yy, my_m], rs.at[2 + my_t]).start()
    left_of(snd.at[pl.ds(0, NI - 1)], ss.at[2])

    load_k.wait()
    load_v.wait()
    eye = iota((HD, HD), 0) == iota((HD, HD), 1)
    for t in range(2):
        local(qin.at[t], qin.at[t], rs.at[2 + t]).wait()
        for e in range(OWN):
            qv = qin[t, :, :, e].reshape(256, HD)
            top = jnp.full((256, 1), NEG, F32)
            acc = jnp.zeros((256, 2 * HD), F32)
            for c in range(KEYS // KC):
                s = dot_t(qv, kk[e, pl.ds(KC * c, KC)])
                part = s[:, :HD]
                for j in range(1, KC // HD):
                    part = jnp.maximum(part, s[:, HD * j : HD * (j + 1)])
                higher = jnp.maximum(top, jnp.max(part, axis=1, keepdims=True))
                p = jnp.exp2(s * C2 - higher * C2)
                again = jnp.exp2((top - higher) * C2)
                acc = acc * again + dot(p.astype(BF16), va[e, pl.ds(KC * c, KC)])
                top = higher
            weight = acc[:, HD:]
            obuf[t, :, :, e] = (acc[:, :HD] / weight).astype(BF16).reshape(2, 8, 16, HD)
            total = top * SCALE + jnp.log(weight)
            for y in range(2):
                tvec[t, y, e] = jnp.sum(
                    jnp.where(eye, total[HD * y : HD * (y + 1)], 0.0), axis=0, keepdims=True
                )
        base = bases[t]
        slots = mid2.at[pl.ds(OWN * inst, OWN)]
        slots_t = tmid.at[pl.ds(OWN * inst, OWN)]

        def back_to(y, z):
            d = y * NZ + z
            remote(obuf.at[t, y, lax.div(z, 2)], slots, ss.at[4], rs.at[4], inst=d).start()

            @pl.when(lax.rem(z, 8) < 2)
            def _():
                remote(tvec.at[t, y], slots_t, ss.at[5], rs.at[5], inst=d).start()

        def back(k, _):
            z = lax.rem(base + 2 * far_first(k, 8), NZ)
            for y in (1 - yy, yy):
                back_to(y, z)
            return 0

        lax.fori_loop(0, 7, back, 0)
        back_to(1 - yy, base)

        @pl.when(my_t == t)
        def _():
            local(obuf.at[t, yy, my_m], slots, rs.at[4]).start()

            @pl.when(has_totals)
            def _():
                local(tvec.at[t, yy], slots_t, rs.at[5]).start()
                local(tvec.at[t, yy], spare.at[pl.ds(BLOCKS // 2, OWN)], ss.at[5]).start()

        @pl.when(my_t != t)
        def _():
            back_to(yy, base)

    left_of(mid2.at[pl.ds(0, OWN * (NI - 1))], ss.at[4])

    left_of(tmid.at[pl.ds(0, OWN * 8)], ss.at[5])

    local(mid2, mid2, rs.at[4]).wait()

    def home(d):
        n0, n1 = lax.div(HALVES * d, 2), lax.div(HALVES * d + 1, 2)
        outer = (n0, n0 + 1), snd2.at[pl.ds(n0, 2)], pin.at[my_t, my_m, pl.ds(0, 2)]
        inner = (n1,), snd2.at[n1], pin.at[my_t, my_m, 2]
        for (blocks, src, dst), parity in ((outer, 0), (inner, 1)):

            @pl.when(lax.rem(d + yy, 2) == parity)
            def _():
                for n in blocks:
                    snd2[n] = mid2[block_slot(n)]

                @pl.when(d == inst)
                def _():
                    local(src, dst, rs.at[6 + my_t]).start()

                @pl.when(d != inst)
                def _():
                    remote(src, dst, ss.at[6], rs.at[6 + my_t], inst=d).start()

    def home_first(z, _):
        for y in (1 - yy, yy):
            home(y * NZ + z)
        return 0

    lax.fori_loop(0, EARLY, home_first, 0)

    def home_others(k, _):
        z = lax.rem(zz + far_first(k, NZ), NZ)

        @pl.when(z >= EARLY)
        def _():
            for y in (1 - yy, yy):
                home(y * NZ + z)

        return 0

    @pl.when(has_totals)
    def _():
        local(tmid, tmid, rs.at[5]).wait()

        def total_home(i, _):
            n = lax.div(my_m, 4) + 2 * i
            tsnd[i] = tmid[block_slot(n)]
            d = lax.div(2 * n + yy, HALVES)
            to = tin.at[my_t, lax.rem(2 * lax.rem(2 * n + yy, HALVES), HALVES)]

            @pl.when(d == inst)
            def _():
                local(tsnd.at[i], to, rs.at[8 + my_t]).start()
                local(tsnd.at[i], spare.at[i], ss.at[7]).start()

            @pl.when(d != inst)
            def _():
                remote(tsnd.at[i], to, ss.at[7], rs.at[8 + my_t], inst=d).start()

            return 0

        lax.fori_loop(0, BLOCKS // 2, total_home, 0)

    lax.fori_loop(0, NZ, home_others, 0)
    left_halves(snd2, ss.at[6])

    def left_totals():
        @pl.when(has_totals)
        def _():
            local(tsnd, tsnd, ss.at[7]).wait()

    left.append(left_totals)

    load_w.wait()
    for t in range(2):
        local(pin.at[t], pin.at[t], rs.at[6 + t]).wait()
        local(tin.at[t], tin.at[t], rs.at[8 + t]).wait()
        for o in range(HALVES):
            total = jnp.sum(
                jnp.where(eye, jnp.broadcast_to(tin[t, o], (HD, HD)), 0.0), axis=1, keepdims=True
            )
            rows = pl.ds(HD * t, HD)
            own_top = own_m[o, rows]
            top = jnp.maximum(total, own_top)
            carried = jnp.exp(total - top)
            own = jnp.exp(own_top - top)
            below = carried + own * own_l[o, rows]
            before = pin[t, :, o].reshape(HD, HD).astype(F32)
            att[t, pl.ds(HD * U_OF[o], HD)] = (carried * before + own * own_acc[o, rows]) / below
        att[t, pl.ds(384, 16)] = jnp.zeros((16, HD), F32)
        for c in range(2):
            for a in range(0, 8, 2):
                for h in range(4):
                    pair = [att[t, pl.ds(24 * (2 * b + c) + h, 8, stride=4)] for b in (a, a + 1)]
                    lhs[t, pl.ds(64 * c + 8 * a, 16), pl.ds(HD * h, HD)] = jnp.concatenate(
                        pair, axis=0
                    ).astype(BF16)
        for c in range(NCH):
            part = dot(lhs[t], w[:, pl.ds(CH * c, CH)])
            cs[t, c] = jnp.where(core == 0, part[64:], part[:64]).astype(BF16)
            mine[t, c] = jnp.where(core == 0, part[:64], part[64:])
            remote(
                cs.at[t, c], cr.at[t, c], css.at[2 * t + c], crs.at[2 * t + c], tp=partner
            ).start()
        for c in range(NCH):
            pair_copy = remote(
                cs.at[t, c], cr.at[t, c], css.at[2 * t + c], crs.at[2 * t + c], tp=partner
            )
            pair_copy.wait_recv()
            left.append(pair_copy.wait_send)
            both = (mine[t, c] + cr[t, c].astype(F32)).reshape(8, 8, CH)
            both = jnp.concatenate([both[:, :, : CH // 2], both[:, :, CH // 2 :]], axis=1)
            sums[t, c] = both
            xs[t, c] = both.astype(BF16)

            def spread_out(n, _):
                remote(
                    xs.at[t, c, lax.rem(chip + n, 8)],
                    xr.at[t, c, n - 1],
                    xss.at[2 * t + c],
                    xrs.at[2 * t + c],
                    tp=chip_at(n),
                ).start()
                return 0

            lax.fori_loop(1, 8, spread_out, 0)
            left_of(xr.at[t, c], xss.at[2 * t + c])
    for wait in left:
        wait()
    for t in range(2):
        for c in range(NCH):
            local(xr.at[t, c], xr.at[t, c], xrs.at[2 * t + c]).wait()
            total = sums[t, c, chip]
            for n in range(7):
                total = total + xr[t, c, n].astype(F32)
            if t == 0:
                step0[c] = total
                continue
            for half in range(2):
                for r in range(6):
                    at = 8 * half + r
                    out[r, :, pl.ds(CH * c + CH // 2 * half, CH // 2)] = jnp.concatenate(
                        [step0[c, pl.ds(at, 1)], total[at : at + 1]], axis=0
                    ).astype(BF16)


def shards(
    queries,
    row_prompt,
    owner_slot,
    suffix_len,
    prefix_keys,
    prefix_values,
    suffix_keys,
    suffix_values,
    new_keys,
    new_values,
    out_weight,
):
    smem = pl.BlockSpec(memory_space=pltpu.SMEM)
    vmem = pl.BlockSpec(memory_space=pltpu.VMEM)
    hbm = pl.BlockSpec(memory_space=pl.ANY)
    sem = pltpu.SemaphoreType.DMA
    scratch = [
        pltpu.VMEM((2, HALVES, 128, HD), BF16),
        pltpu.VMEM((OWN, KEYS, HD), BF16),
        pltpu.VMEM((OWN, KEYS, 2 * HD), BF16),
        pltpu.VMEM((HALVES, 384, HD), BF16),
        pltpu.VMEM((HALVES, 384, HD), BF16),
        pltpu.VMEM((512, D), BF16),
        pltpu.VMEM((NI, 1, HD), I32),
        pltpu.VMEM((1, HD), I32),
        pltpu.SMEM((1, HD), I32),
        pltpu.VMEM((BLOCKS, 16, HD), BF16),
        pltpu.VMEM((NI, OWN, 16, HD), BF16),
        pltpu.VMEM((2, 2, 8, OWN, 16, HD), BF16),
        pltpu.VMEM((2, 2, 8, OWN, 16, HD), BF16),
        pltpu.VMEM((SLOTS, 16, HD), BF16),
        pltpu.VMEM((BLOCKS, 16, HD), BF16),
        pltpu.VMEM((2, 8, HALVES, 16, HD), BF16),
        pltpu.VMEM((2, 2, OWN, 1, HD), F32),
        pltpu.VMEM((SLOTS, 1, HD), F32),
        pltpu.VMEM((BLOCKS // 2, 1, HD), F32),
        pltpu.VMEM((BLOCKS // 2 + OWN, 1, HD), F32),
        pltpu.VMEM((2, HALVES, 1, HD), F32),
        pltpu.VMEM((HALVES, 256, HD), F32),
        pltpu.VMEM((HALVES, 256, HD), F32),
        pltpu.VMEM((HALVES, 256, HD), F32),
        pltpu.VMEM((2, 400, HD), F32),
        pltpu.VMEM((2, 128, 512), BF16),
        pltpu.VMEM((2, NCH, 64, CH), F32),
        pltpu.VMEM((2, NCH, 64, CH), BF16),
        pltpu.VMEM((2, NCH, 64, CH), BF16),
        pltpu.VMEM((2, NCH, 8, 16, CH // 2), BF16),
        pltpu.VMEM((2, NCH, 7, 16, CH // 2), BF16),
        pltpu.VMEM((2, NCH, 8, 16, CH // 2), F32),
        pltpu.VMEM((NCH, 16, CH // 2), F32),
        sem((17,)),
        sem((8,)),
        sem((10,)),
        sem((2 * NCH,)),
        sem((2 * NCH,)),
        sem((2 * NCH,)),
        sem((2 * NCH,)),
    ]
    return pl.pallas_call(
        kernel,
        out_shape=jax.ShapeDtypeStruct((6, 2, D), BF16),
        in_specs=[smem, smem, vmem] + [hbm] * 8,
        out_specs=vmem,
        scratch_shapes=scratch,
        compiler_params=pltpu.CompilerParams(
            collective_id=0, has_side_effects=True, vmem_limit_bytes=56 * 1024 * 1024
        ),
    )(
        row_prompt,
        owner_slot,
        suffix_len.reshape(1, 96),
        queries.reshape(2, 384, HD),
        prefix_keys.reshape(OWN, KEYS, HD),
        prefix_values.reshape(OWN, KEYS, HD),
        suffix_keys.reshape(768, HD),
        suffix_values.reshape(768, HD),
        new_keys.reshape(2, 96, HD),
        new_values.reshape(2, 96, HD),
        out_weight,
    )


def solution(mesh):
    placed = (
        P(None, "inst", "tp", None),
        P("inst"),
        P(),
        P("inst"),
        P("inst", None, "tp", None),
        P("inst", None, "tp", None),
        P("inst", None, "tp", None),
        P("inst", None, "tp", None),
        P(None, "inst", "tp", None),
        P(None, "inst", "tp", None),
        P("tp", None),
    )
    return jax.shard_map(
        shards, mesh=mesh, in_specs=placed, out_specs=P(("inst", "tp"), None, None), check_vma=False
    )
```

```python
import math

import jax
import jax.numpy as jnp
from jax import lax
from jax.experimental import pallas as pl
from jax.experimental.pallas import tpu as pltpu
from jax.sharding import PartitionSpec as P

F32 = jnp.float32
BF16 = jnp.bfloat16
I32 = jnp.int32

NI = 32
NZ = 16
HALVES = 3
BLOCKS = 48
SLOTS = 64
CHIPS = ((2, 1), (2, 0), (1, 1), (3, 1), (1, 0), (3, 0), (0, 1))
EARLY = 4
OWN = 2
HD = 128
KEYS = 4096
D = 2560
CH = 1280
NCH = D // CH
PK = 512
KC = 1024
U_OF = (0, 2, 1)
SCALE = 1.0 / math.sqrt(HD)
C2 = SCALE * math.log2(math.e)
NEG = -1e30


def dot_t(a, b):
    return lax.dot_general(a, b, (((1,), (1,)), ((), ())), preferred_element_type=F32)


def dot(a, b):
    return lax.dot_general(a, b, (((1,), (0,)), ((), ())), preferred_element_type=F32)


def iota(shape, dim):
    return lax.broadcasted_iota(I32, shape, dim)


def far_first(k, n):
    up = lax.rem(k + 1, 2)
    return lax.rem(n // 2 + up * lax.div(k, 2) + (1 - up) * (n - lax.div(k + 1, 2)), n)


def kernel(
    rp_hbm,
    os_hbm,
    lens_hbm,
    q_hbm,
    k_hbm,
    v_hbm,
    sk_hbm,
    sv_hbm,
    nk_hbm,
    nv_hbm,
    w_hbm,
    out,
    row_prompt,
    owner_slot,
    lens,
    q,
    kk,
    va,
    ck,
    cv,
    w,
    tab,
    inv_v,
    inv_s,
    mid,
    snd,
    qin,
    obuf,
    mid2,
    snd2,
    pin,
    tvec,
    tmid,
    tsnd,
    spare,
    tin,
    own_acc,
    own_m,
    own_l,
    att,
    lhs,
    mine,
    cs,
    cr,
    xs,
    xr,
    sums,
    step0,
    ld,
    ss,
    rs,
    css,
    crs,
    xss,
    xrs,
):
    inst = lax.axis_index("inst")
    tp = lax.axis_index("tp")
    yy = lax.div(inst, NZ)
    zz = lax.rem(inst, NZ)
    core = lax.rem(tp, 2)
    chip = lax.div(tp, 2)
    partner = tp + 1 - 2 * core
    my_t = lax.rem(zz, 2)
    my_m = lax.div(zz, 2)
    has_totals = lax.rem(zz, 8) < 2

    def remote(src, dst, s, r, **where):
        return pltpu.make_async_remote_copy(
            src_ref=src, dst_ref=dst, send_sem=s, recv_sem=r,
            device_id=where, device_id_type=pl.DeviceIdType.MESH,
        )

    def local(src, dst, s):
        return pltpu.make_async_copy(src, dst, s)

    def chip_at(step):
        return lax.rem(chip + step, 8) * 2 + core

    left = []

    def left_of(ref, sem):
        left.append(lambda: local(ref, ref, sem).wait())

    barrier = pltpu.get_barrier_semaphore()

    def greet(k, _):
        z = lax.rem(zz + far_first(k, NZ), NZ)
        for y in (1 - yy, yy):
            pl.semaphore_signal(
                barrier, inc=1, device_id={"inst": y * NZ + z},
                device_id_type=pl.DeviceIdType.MESH,
            )
        return 0

    lax.fori_loop(0, NZ - 1, greet, 0)
    pl.semaphore_signal(
        barrier, inc=1, device_id={"inst": (1 - yy) * NZ + zz}, device_id_type=pl.DeviceIdType.MESH
    )

    def greet_chip(n, _):
        pl.semaphore_signal(
            barrier, inc=1, device_id={"tp": chip_at(n)}, device_id_type=pl.DeviceIdType.MESH
        )
        return 0

    lax.fori_loop(1, 8, greet_chip, 0)
    pl.semaphore_signal(
        barrier, inc=1, device_id={"tp": partner}, device_id_type=pl.DeviceIdType.MESH
    )

    loads_t = [
        local(rp_hbm, row_prompt, ld.at[17]),
        local(os_hbm, owner_slot, ld.at[18]),
    ]
    for c in loads_t:
        c.start()
    loads_q = [
        local(q_hbm.at[:, pl.ds(128 * U_OF[o], 128)], q.at[:, o], ld.at[0]) for o in range(HALVES)
    ]
    for c in loads_q:
        c.start()
    loads_own = []
    for o in range(HALVES):
        u = U_OF[o]
        for src, dst, sem in ((sk_hbm, ck, 3), (sv_hbm, cv, 4)):
            loads_own.append(
                local(src.at[pl.ds(256 * u, 256)], dst.at[o, pl.ds(0, 256)], ld.at[sem + 4 * o])
            )
        for src, dst, sem in ((nk_hbm, ck, 5), (nv_hbm, cv, 6)):
            loads_own.append(
                local(
                    src.at[:, pl.ds(32 * u, 32)],
                    dst.at[o, pl.ds(256, 64)].reshape(2, 32, HD),
                    ld.at[sem + 4 * o],
                )
            )
    loads_own.append(local(lens_hbm, lens, ld.at[19]))
    for c in loads_own:
        c.start()
    load_k = local(k_hbm, kk, ld.at[1])
    load_k.start()
    load_v = local(v_hbm, va.at[:, :, pl.ds(0, HD)], ld.at[2])
    load_v.start()
    load_w = local(w_hbm, w, ld.at[15])
    load_w.start()

    for c in loads_t:
        c.wait()
    lane1 = iota((1, HD), 1)
    head = jnp.zeros((1, HD), I32)
    for u in range(HALVES):
        block = lax.div(HALVES * inst + u, 2)
        first = lax.rem(HALVES * inst + u, 2) == 0
        slot = owner_slot[row_prompt[32 * u]]
        head += jnp.where((lane1 == slot) & first, block, 0)
        head += jnp.where((lane1 == SLOTS + block) & first, slot, 0)
    tab[inst] = head
    ones = jnp.ones((256, HD), BF16)

    def set_ones(n, _):
        va[lax.div(n, 16), pl.ds(pl.multiple_of(lax.rem(n, 16) * 256, 256), 256), pl.ds(HD, HD)] = ones
        return 0

    lax.fori_loop(0, 32, set_ones, 0)
    for o in range(HALVES):
        ck[o, pl.ds(320, 64)] = jnp.zeros((64, HD), BF16)
        cv[o, pl.ds(320, 64)] = jnp.zeros((64, HD), BF16)
    for c in loads_q:
        c.wait()

    pl.semaphore_wait(barrier, NI - 1 + 1 + 7)

    b_outer = lax.div(HALVES * inst, 2)
    b_inner = lax.div(HALVES * inst + 1, 2)
    side_outer = lax.rem(zz, 2)
    side_inner = 1 - side_outer

    def outer_piece(z):
        at = pl.ds(pl.multiple_of(16 * lax.div(z, 2), 16), 16)
        return q.at[lax.rem(z, 2), pl.ds(0, 2), at], mid.at[pl.ds(b_outer, 2)]

    def inner_piece(z):
        at = pl.ds(pl.multiple_of(16 * lax.div(z, 2), 16), 16)
        return q.at[lax.rem(z, 2), 2, at], mid.at[b_inner]

    def send_head(d):
        remote(tab.at[inst], tab.at[inst], ss.at[0], rs.at[0], inst=d).start()

    def send_pieces(z):
        send_head(side_outer * NZ + z)
        send_head(side_inner * NZ + z)
        remote(*outer_piece(z), ss.at[1], rs.at[1], inst=side_outer * NZ + z).start()
        remote(*inner_piece(z), ss.at[1], rs.at[1], inst=side_inner * NZ + z).start()

    bases = [lax.rem(zz + lax.rem(zz + t, 2), NZ) for t in range(2)]
    across = (1 - yy) * NZ + zz
    for t in range(2):

        def send_step(k, _):
            send_pieces(lax.rem(bases[t] + 2 * far_first(k, 8), NZ))
            return 0

        lax.fori_loop(0, 7, send_step, 0)

        @pl.when(my_t != t)
        def _():
            send_pieces(bases[t])

        @pl.when((my_t == t) & (side_outer == yy))
        def _():
            send_head(across)
            local(*outer_piece(zz), rs.at[1]).start()
            remote(*inner_piece(zz), ss.at[1], rs.at[1], inst=across).start()

        @pl.when((my_t == t) & (side_outer != yy))
        def _():
            send_head(across)
            local(*inner_piece(zz), rs.at[1]).start()
            remote(*outer_piece(zz), ss.at[1], rs.at[1], inst=across).start()

    heads_all = tab.at[pl.ds(0, NI - 1)]
    left_of(heads_all, ss.at[0])
    kept_here = 1 + jnp.where(side_outer == yy, 1, 0)

    def left_halves(ref, sem):
        def wait():
            for n_kept in (1, 2):

                @pl.when(kept_here == n_kept)
                def _():
                    sent = ref.at[pl.ds(0, BLOCKS - n_kept)]
                    local(sent, sent, sem).wait()

        left.append(wait)

    left_halves(mid, ss.at[1])

    for c in loads_own:
        c.wait()
    lens_b = jnp.broadcast_to(lens[...].astype(F32), (8, 96)).astype(BF16)
    for o in range(HALVES):
        u = U_OF[o]
        at96 = iota((96, 384), 0)
        lane96 = iota((96, 384), 1)
        spread = jnp.where(at96 == 32 * u + lax.div(lane96, 8), 1.0, 0.0).astype(BF16)
        len_row = dot(lens_b, spread)[0:1]
        row = iota((256, 384), 0)
        lane = iota((256, 384), 1)
        sample = lax.div(lax.rem(row, 128), 4)
        step = lax.div(row, 128)
        cached = (lane < 256) & (lax.div(lane, 8) == sample) & (
            lax.rem(lane, 8).astype(F32) < jnp.broadcast_to(len_row, (256, 384))
        )
        new_at = lane - 256
        new = (lane >= 256) & (lane < 320) & (lax.rem(new_at, 32) == sample) & (
            lax.div(new_at, 32) <= step
        )
        qu = jnp.concatenate([q[0, o], q[1, o]], axis=0)
        s = jnp.where(cached | new, dot_t(qu, ck[o]), NEG)
        top = jnp.max(s, axis=1, keepdims=True)
        p = jnp.exp2(s * C2 - top * C2)
        own_m[o] = jnp.broadcast_to(top * SCALE, (256, HD))
        own_l[o] = jnp.broadcast_to(jnp.sum(p, axis=1, keepdims=True), (256, HD))
        own_acc[o] = dot(p.astype(BF16), cv[o])

    local(heads_all, heads_all, rs.at[0]).wait()
    inv_v[...] = jnp.sum(tab[...], axis=0)
    to_smem = local(inv_v, inv_s, ld.at[16])
    to_smem.start()
    to_smem.wait()

    def slot_block(s):
        return jnp.clip(inv_s[0, s], 0, BLOCKS - 1)

    def block_slot(n):
        return jnp.clip(inv_s[0, SLOTS + n], 0, SLOTS - 1)

    local(mid, mid, rs.at[1]).wait()

    def select(d):
        for e in range(OWN):
            snd[d, e] = mid[slot_block(OWN * d + e)]

    def to_owner(d):
        return remote(snd.at[d], qin.at[my_t, yy, my_m], ss.at[2], rs.at[2 + my_t], inst=d)

    def send_selected(k, _):
        z = lax.rem(zz + far_first(k, NZ), NZ)
        for y in (1 - yy, yy):
            d = y * NZ + z
            select(d)
            to_owner(d).start()
        return 0

    lax.fori_loop(0, NZ - 1, send_selected, 0)
    select(across)
    to_owner(across).start()
    select(inst)
    local(snd.at[inst], qin.at[my_t, yy, my_m], rs.at[2 + my_t]).start()
    left_of(snd.at[pl.ds(0, NI - 1)], ss.at[2])

    load_k.wait()
    load_v.wait()
    eye = iota((HD, HD), 0) == iota((HD, HD), 1)
    for t in range(2):
        local(qin.at[t], qin.at[t], rs.at[2 + t]).wait()
        for e in range(OWN):
            qv = qin[t, :, :, e].reshape(256, HD)
            top = jnp.full((256, 1), NEG, F32)
            acc = jnp.zeros((256, 2 * HD), F32)
            for c in range(KEYS // KC):
                s = dot_t(qv, kk[e, pl.ds(KC * c, KC)])
                part = s[:, :HD]
                for j in range(1, KC // HD):
                    part = jnp.maximum(part, s[:, HD * j : HD * (j + 1)])
                higher = jnp.maximum(top, jnp.max(part, axis=1, keepdims=True))
                p = jnp.exp2(s * C2 - higher * C2)
                again = jnp.exp2((top - higher) * C2)
                acc = acc * again + dot(p.astype(BF16), va[e, pl.ds(KC * c, KC)])
                top = higher
            weight = acc[:, HD:]
            obuf[t, :, :, e] = (acc[:, :HD] / weight).astype(BF16).reshape(2, 8, 16, HD)
            total = top * SCALE + jnp.log(weight)
            for y in range(2):
                tvec[t, y, e] = jnp.sum(
                    jnp.where(eye, total[HD * y : HD * (y + 1)], 0.0), axis=0, keepdims=True
                )
        base = bases[t]
        slots = mid2.at[pl.ds(OWN * inst, OWN)]
        slots_t = tmid.at[pl.ds(OWN * inst, OWN)]

        def back_to(y, z):
            d = y * NZ + z
            remote(obuf.at[t, y, lax.div(z, 2)], slots, ss.at[4], rs.at[4], inst=d).start()

            @pl.when(lax.rem(z, 8) < 2)
            def _():
                remote(tvec.at[t, y], slots_t, ss.at[5], rs.at[5], inst=d).start()

        def back(k, _):
            z = lax.rem(base + 2 * far_first(k, 8), NZ)
            for y in (1 - yy, yy):
                back_to(y, z)
            return 0

        lax.fori_loop(0, 7, back, 0)
        back_to(1 - yy, base)

        @pl.when(my_t == t)
        def _():
            local(obuf.at[t, yy, my_m], slots, rs.at[4]).start()

            @pl.when(has_totals)
            def _():
                local(tvec.at[t, yy], slots_t, rs.at[5]).start()
                local(tvec.at[t, yy], spare.at[pl.ds(BLOCKS // 2, OWN)], ss.at[5]).start()

        @pl.when(my_t != t)
        def _():
            back_to(yy, base)

    left_of(mid2.at[pl.ds(0, OWN * (NI - 1))], ss.at[4])

    left_of(tmid.at[pl.ds(0, OWN * 8)], ss.at[5])

    local(mid2, mid2, rs.at[4]).wait()

    def home(d):
        n0, n1 = lax.div(HALVES * d, 2), lax.div(HALVES * d + 1, 2)
        outer = (n0, n0 + 1), snd2.at[pl.ds(n0, 2)], pin.at[my_t, my_m, pl.ds(0, 2)]
        inner = (n1,), snd2.at[n1], pin.at[my_t, my_m, 2]
        for (blocks, src, dst), parity in ((outer, 0), (inner, 1)):

            @pl.when(lax.rem(d + yy, 2) == parity)
            def _():
                for n in blocks:
                    snd2[n] = mid2[block_slot(n)]

                @pl.when(d == inst)
                def _():
                    local(src, dst, rs.at[6 + my_t]).start()

                @pl.when(d != inst)
                def _():
                    remote(src, dst, ss.at[6], rs.at[6 + my_t], inst=d).start()

    def home_first(z, _):
        for y in (1 - yy, yy):
            home(y * NZ + z)
        return 0

    lax.fori_loop(0, EARLY, home_first, 0)

    def home_others(k, _):
        z = lax.rem(zz + far_first(k, NZ), NZ)

        @pl.when(z >= EARLY)
        def _():
            for y in (1 - yy, yy):
                home(y * NZ + z)

        return 0

    @pl.when(has_totals)
    def _():
        local(tmid, tmid, rs.at[5]).wait()

        def total_home(i, _):
            n = lax.div(my_m, 4) + 2 * i
            tsnd[i] = tmid[block_slot(n)]
            d = lax.div(2 * n + yy, HALVES)
            to = tin.at[my_t, lax.rem(2 * lax.rem(2 * n + yy, HALVES), HALVES)]

            @pl.when(d == inst)
            def _():
                local(tsnd.at[i], to, rs.at[8 + my_t]).start()
                local(tsnd.at[i], spare.at[i], ss.at[7]).start()

            @pl.when(d != inst)
            def _():
                remote(tsnd.at[i], to, ss.at[7], rs.at[8 + my_t], inst=d).start()

            return 0

        lax.fori_loop(0, BLOCKS // 2, total_home, 0)

    lax.fori_loop(0, NZ, home_others, 0)
    left_halves(snd2, ss.at[6])

    def left_totals():
        @pl.when(has_totals)
        def _():
            local(tsnd, tsnd, ss.at[7]).wait()

    left.append(left_totals)

    load_w.wait()
    for t in range(2):
        local(pin.at[t], pin.at[t], rs.at[6 + t]).wait()
        local(tin.at[t], tin.at[t], rs.at[8 + t]).wait()
        for o in range(HALVES):
            total = jnp.sum(
                jnp.where(eye, jnp.broadcast_to(tin[t, o], (HD, HD)), 0.0), axis=1, keepdims=True
            )
            rows = pl.ds(HD * t, HD)
            own_top = own_m[o, rows]
            top = jnp.maximum(total, own_top)
            carried = jnp.exp(total - top)
            own = jnp.exp(own_top - top)
            below = carried + own * own_l[o, rows]
            before = pin[t, :, o].reshape(HD, HD).astype(F32)
            att[t, pl.ds(HD * U_OF[o], HD)] = (carried * before + own * own_acc[o, rows]) / below
        att[t, pl.ds(384, 16)] = jnp.zeros((16, HD), F32)
        for c in range(2):
            for a in range(0, 8, 2):
                for h in range(4):
                    pair = [att[t, pl.ds(24 * (2 * b + c) + h, 8, stride=4)] for b in (a, a + 1)]
                    lhs[t, pl.ds(64 * c + 8 * a, 16), pl.ds(HD * h, HD)] = jnp.concatenate(
                        pair, axis=0
                    ).astype(BF16)
        for c in range(NCH):
            part = dot(lhs[t], w[:, pl.ds(CH * c, CH)])
            cs[t, c] = jnp.where(core == 0, part[64:], part[:64]).astype(BF16)
            mine[t, c] = jnp.where(core == 0, part[:64], part[64:])
            remote(
                cs.at[t, c], cr.at[t, c], css.at[2 * t + c], crs.at[2 * t + c], tp=partner
            ).start()
        for c in range(NCH):
            pair_copy = remote(
                cs.at[t, c], cr.at[t, c], css.at[2 * t + c], crs.at[2 * t + c], tp=partner
            )
            pair_copy.wait_recv()
            left.append(pair_copy.wait_send)
            both = (mine[t, c] + cr[t, c].astype(F32)).reshape(8, 8, CH)
            rest = both[:, :, 2 * PK :]
            rest = jnp.concatenate([rest[:, :4], rest[:, 4:8]], axis=2)
            both = jnp.concatenate([both[:, :6, :PK], both[:, :6, PK : 2 * PK], rest], axis=1)
            sums[t, c] = both
            xs[t, c] = both.astype(BF16)

            for n, (dx, dy) in enumerate(CHIPS):
                to = lax.rem(lax.div(chip, 2) + dx, 4) * 2 + lax.rem(chip + dy, 2)
                remote(
                    xs.at[t, c, to],
                    xr.at[t, c, n],
                    xss.at[2 * t + c],
                    xrs.at[2 * t + c],
                    tp=2 * to + core,
                ).start()
            left_of(xr.at[t, c], xss.at[2 * t + c])
    for wait in left:
        wait()
    for t in range(2):
        for c in range(NCH):
            local(xr.at[t, c], xr.at[t, c], xrs.at[2 * t + c]).wait()
            total = sums[t, c, chip]
            for n in range(7):
                total = total + xr[t, c, n].astype(F32)
            if t == 0:
                step0[c] = total
                continue
            for r in range(6):
                last = (12 + r, 0) if r < 4 else (8 + r, PK // 2)
                for at, lane, to, width in (
                    (r, 0, 0, PK),
                    (6 + r, 0, PK, PK),
                    (*last, 2 * PK, PK // 2),
                ):
                    out[r, :, pl.ds(CH * c + to, width)] = jnp.concatenate(
                        [
                            step0[c, pl.ds(at, 1), pl.ds(lane, width)],
                            total[at : at + 1, lane : lane + width],
                        ],
                        axis=0,
                    ).astype(BF16)


def shards(
    queries,
    row_prompt,
    owner_slot,
    suffix_len,
    prefix_keys,
    prefix_values,
    suffix_keys,
    suffix_values,
    new_keys,
    new_values,
    out_weight,
):
    vmem = pl.BlockSpec(memory_space=pltpu.VMEM)
    hbm = pl.BlockSpec(memory_space=pl.ANY)
    sem = pltpu.SemaphoreType.DMA
    scratch = [
        pltpu.SMEM((96,), I32),
        pltpu.SMEM((48,), I32),
        pltpu.VMEM((1, 96), I32),
        pltpu.VMEM((2, HALVES, 128, HD), BF16),
        pltpu.VMEM((OWN, KEYS, HD), BF16),
        pltpu.VMEM((OWN, KEYS, 2 * HD), BF16),
        pltpu.VMEM((HALVES, 384, HD), BF16),
        pltpu.VMEM((HALVES, 384, HD), BF16),
        pltpu.VMEM((512, D), BF16),
        pltpu.VMEM((NI, 1, HD), I32),
        pltpu.VMEM((1, HD), I32),
        pltpu.SMEM((1, HD), I32),
        pltpu.VMEM((BLOCKS, 16, HD), BF16),
        pltpu.VMEM((NI, OWN, 16, HD), BF16),
        pltpu.VMEM((2, 2, 8, OWN, 16, HD), BF16),
        pltpu.VMEM((2, 2, 8, OWN, 16, HD), BF16),
        pltpu.VMEM((SLOTS, 16, HD), BF16),
        pltpu.VMEM((BLOCKS, 16, HD), BF16),
        pltpu.VMEM((2, 8, HALVES, 16, HD), BF16),
        pltpu.VMEM((2, 2, OWN, 1, HD), F32),
        pltpu.VMEM((SLOTS, 1, HD), F32),
        pltpu.VMEM((BLOCKS // 2, 1, HD), F32),
        pltpu.VMEM((BLOCKS // 2 + OWN, 1, HD), F32),
        pltpu.VMEM((2, HALVES, 1, HD), F32),
        pltpu.VMEM((HALVES, 256, HD), F32),
        pltpu.VMEM((HALVES, 256, HD), F32),
        pltpu.VMEM((HALVES, 256, HD), F32),
        pltpu.VMEM((2, 400, HD), F32),
        pltpu.VMEM((2, 128, 512), BF16),
        pltpu.VMEM((2, NCH, 64, CH), F32),
        pltpu.VMEM((2, NCH, 64, CH), BF16),
        pltpu.VMEM((2, NCH, 64, CH), BF16),
        pltpu.VMEM((2, NCH, 8, 16, PK), BF16),
        pltpu.VMEM((2, NCH, 7, 16, PK), BF16),
        pltpu.VMEM((2, NCH, 8, 16, PK), F32),
        pltpu.VMEM((NCH, 16, PK), F32),
        sem((20,)),
        sem((8,)),
        sem((10,)),
        sem((2 * NCH,)),
        sem((2 * NCH,)),
        sem((2 * NCH,)),
        sem((2 * NCH,)),
    ]
    return pl.pallas_call(
        kernel,
        out_shape=jax.ShapeDtypeStruct((6, 2, D), BF16),
        in_specs=[hbm] * 11,
        out_specs=vmem,
        scratch_shapes=scratch,
        compiler_params=pltpu.CompilerParams(
            collective_id=0, has_side_effects=True, vmem_limit_bytes=56 * 1024 * 1024
        ),
    )(
        row_prompt,
        owner_slot,
        suffix_len.reshape(1, 96),
        queries.reshape(2, 384, HD),
        prefix_keys.reshape(OWN, KEYS, HD),
        prefix_values.reshape(OWN, KEYS, HD),
        suffix_keys.reshape(768, HD),
        suffix_values.reshape(768, HD),
        new_keys.reshape(2, 96, HD),
        new_values.reshape(2, 96, HD),
        out_weight,
    )


def solution(mesh):
    placed = (
        P(None, "inst", "tp", None),
        P("inst"),
        P(),
        P("inst"),
        P("inst", None, "tp", None),
        P("inst", None, "tp", None),
        P("inst", None, "tp", None),
        P("inst", None, "tp", None),
        P(None, "inst", "tp", None),
        P(None, "inst", "tp", None),
        P("tp", None),
    )
    return jax.shard_map(
        shards, mesh=mesh, in_specs=placed, out_specs=P(("inst", "tp"), None, None), check_vma=False
    )
```

```python
import math

import jax
import jax.numpy as jnp
from jax import lax
from jax.experimental import pallas as pl
from jax.experimental.pallas import tpu as pltpu
from jax.sharding import PartitionSpec as P

F32 = jnp.float32
BF16 = jnp.bfloat16
I32 = jnp.int32

NI = 32
NZ = 16
HALVES = 3
BLOCKS = 48
SLOTS = 64
CHIPS = ((2, 1), (2, 0), (1, 1), (3, 1), (1, 0), (3, 0), (0, 1))
EARLY = 4
OWN = 2
HD = 128
KEYS = 4096
D = 2560
CH = 1280
NCH = D // CH
PK = 512
KC = 1024
U_OF = (0, 2, 1)
SCALE = 1.0 / math.sqrt(HD)
C2 = SCALE * math.log2(math.e)
NEG = -1e30


def dot_t(a, b):
    return lax.dot_general(a, b, (((1,), (1,)), ((), ())), preferred_element_type=F32)


def dot(a, b):
    return lax.dot_general(a, b, (((1,), (0,)), ((), ())), preferred_element_type=F32)


def iota(shape, dim):
    return lax.broadcasted_iota(I32, shape, dim)


def far_first(k, n):
    up = lax.rem(k + 1, 2)
    return lax.rem(n // 2 + up * lax.div(k, 2) + (1 - up) * (n - lax.div(k + 1, 2)), n)


def kernel(
    rp_hbm,
    os_hbm,
    lens_hbm,
    q_hbm,
    k_hbm,
    v_hbm,
    sk_hbm,
    sv_hbm,
    nk_hbm,
    nv_hbm,
    w_hbm,
    out,
    row_prompt,
    owner_slot,
    lens,
    q,
    kk,
    va,
    ck,
    cv,
    w,
    tab,
    inv_v,
    inv_s,
    mid,
    snd,
    qin,
    obuf,
    mid2,
    snd2,
    pin,
    tvec,
    tmid,
    tsnd,
    spare,
    tin,
    own_acc,
    own_m,
    own_l,
    att,
    lhs,
    mine,
    cs,
    cr,
    xs,
    xr,
    sums,
    step0,
    ld,
    ss,
    rs,
    css,
    crs,
    xss,
    xrs,
):
    inst = lax.axis_index("inst")
    tp = lax.axis_index("tp")
    yy = lax.div(inst, NZ)
    zz = lax.rem(inst, NZ)
    core = lax.rem(tp, 2)
    chip = lax.div(tp, 2)
    partner = tp + 1 - 2 * core
    my_t = lax.rem(zz, 2)
    my_m = lax.div(zz, 2)
    has_totals = lax.rem(zz, 8) < 4

    def remote(src, dst, s, r, **where):
        return pltpu.make_async_remote_copy(
            src_ref=src, dst_ref=dst, send_sem=s, recv_sem=r,
            device_id=where, device_id_type=pl.DeviceIdType.MESH,
        )

    def local(src, dst, s):
        return pltpu.make_async_copy(src, dst, s)

    def chip_at(step):
        return lax.rem(chip + step, 8) * 2 + core

    left = []

    def left_of(ref, sem):
        left.append(lambda: local(ref, ref, sem).wait())

    barrier = pltpu.get_barrier_semaphore()

    def greet(k, _):
        z = lax.rem(zz + far_first(k, NZ), NZ)
        for y in (1 - yy, yy):
            pl.semaphore_signal(
                barrier, inc=1, device_id={"inst": y * NZ + z},
                device_id_type=pl.DeviceIdType.MESH,
            )
        return 0

    lax.fori_loop(0, NZ - 1, greet, 0)
    pl.semaphore_signal(
        barrier, inc=1, device_id={"inst": (1 - yy) * NZ + zz}, device_id_type=pl.DeviceIdType.MESH
    )

    def greet_chip(n, _):
        pl.semaphore_signal(
            barrier, inc=1, device_id={"tp": chip_at(n)}, device_id_type=pl.DeviceIdType.MESH
        )
        return 0

    lax.fori_loop(1, 8, greet_chip, 0)
    pl.semaphore_signal(
        barrier, inc=1, device_id={"tp": partner}, device_id_type=pl.DeviceIdType.MESH
    )

    loads_t = [
        local(rp_hbm, row_prompt, ld.at[17]),
        local(os_hbm, owner_slot, ld.at[18]),
    ]
    for c in loads_t:
        c.start()
    loads_q = [
        local(q_hbm.at[:, pl.ds(128 * U_OF[o], 128)], q.at[:, o], ld.at[0]) for o in range(HALVES)
    ]
    for c in loads_q:
        c.start()
    loads_own = []
    for o in range(HALVES):
        u = U_OF[o]
        for src, dst, sem in ((sk_hbm, ck, 3), (sv_hbm, cv, 4)):
            loads_own.append(
                local(src.at[pl.ds(256 * u, 256)], dst.at[o, pl.ds(0, 256)], ld.at[sem + 4 * o])
            )
        for src, dst, sem in ((nk_hbm, ck, 5), (nv_hbm, cv, 6)):
            loads_own.append(
                local(
                    src.at[:, pl.ds(32 * u, 32)],
                    dst.at[o, pl.ds(256, 64)].reshape(2, 32, HD),
                    ld.at[sem + 4 * o],
                )
            )
    loads_own.append(local(lens_hbm, lens, ld.at[19]))
    for c in loads_own:
        c.start()
    load_k = local(k_hbm, kk, ld.at[1])
    load_k.start()
    load_v = local(v_hbm, va.at[:, :, pl.ds(0, HD)], ld.at[2])
    load_v.start()
    load_w = local(w_hbm, w, ld.at[15])
    load_w.start()

    for c in loads_t:
        c.wait()
    lane1 = iota((1, HD), 1)
    head = jnp.zeros((1, HD), I32)
    for u in range(HALVES):
        block = lax.div(HALVES * inst + u, 2)
        first = lax.rem(HALVES * inst + u, 2) == 0
        slot = owner_slot[row_prompt[32 * u]]
        head += jnp.where((lane1 == slot) & first, block, 0)
        head += jnp.where((lane1 == SLOTS + block) & first, slot, 0)
    tab[inst] = head
    ones = jnp.ones((256, HD), BF16)

    def set_ones(n, _):
        va[lax.div(n, 16), pl.ds(pl.multiple_of(lax.rem(n, 16) * 256, 256), 256), pl.ds(HD, HD)] = ones
        return 0

    lax.fori_loop(0, 32, set_ones, 0)
    for o in range(HALVES):
        ck[o, pl.ds(320, 64)] = jnp.zeros((64, HD), BF16)
        cv[o, pl.ds(320, 64)] = jnp.zeros((64, HD), BF16)
    for c in loads_q:
        c.wait()

    pl.semaphore_wait(barrier, NI - 1 + 1 + 7)

    b_outer = lax.div(HALVES * inst, 2)
    b_inner = lax.div(HALVES * inst + 1, 2)
    side_outer = lax.rem(zz, 2)
    side_inner = 1 - side_outer

    def outer_piece(z):
        at = pl.ds(pl.multiple_of(16 * lax.div(z, 2), 16), 16)
        return q.at[lax.rem(z, 2), pl.ds(0, 2), at], mid.at[pl.ds(b_outer, 2)]

    def inner_piece(z):
        at = pl.ds(pl.multiple_of(16 * lax.div(z, 2), 16), 16)
        return q.at[lax.rem(z, 2), 2, at], mid.at[b_inner]

    def send_head(d):
        remote(tab.at[inst], tab.at[inst], ss.at[0], rs.at[0], inst=d).start()

    def send_pieces(z):
        send_head(side_outer * NZ + z)
        send_head(side_inner * NZ + z)
        remote(*outer_piece(z), ss.at[1], rs.at[1], inst=side_outer * NZ + z).start()
        remote(*inner_piece(z), ss.at[1], rs.at[1], inst=side_inner * NZ + z).start()

    bases = [lax.rem(zz + lax.rem(zz + t, 2), NZ) for t in range(2)]
    across = (1 - yy) * NZ + zz
    for t in range(2):

        def send_step(k, _):
            send_pieces(lax.rem(bases[t] + 2 * far_first(k, 8), NZ))
            return 0

        lax.fori_loop(0, 7, send_step, 0)

        @pl.when(my_t != t)
        def _():
            send_pieces(bases[t])

        @pl.when((my_t == t) & (side_outer == yy))
        def _():
            send_head(across)
            local(*outer_piece(zz), rs.at[1]).start()
            remote(*inner_piece(zz), ss.at[1], rs.at[1], inst=across).start()

        @pl.when((my_t == t) & (side_outer != yy))
        def _():
            send_head(across)
            local(*inner_piece(zz), rs.at[1]).start()
            remote(*outer_piece(zz), ss.at[1], rs.at[1], inst=across).start()

    heads_all = tab.at[pl.ds(0, NI - 1)]
    left_of(heads_all, ss.at[0])
    kept_here = 1 + jnp.where(side_outer == yy, 1, 0)

    def left_halves(ref, sem):
        def wait():
            for n_kept in (1, 2):

                @pl.when(kept_here == n_kept)
                def _():
                    sent = ref.at[pl.ds(0, BLOCKS - n_kept)]
                    local(sent, sent, sem).wait()

        left.append(wait)

    left_halves(mid, ss.at[1])

    for c in loads_own:
        c.wait()
    lens_b = jnp.broadcast_to(lens[...].astype(F32), (8, 96)).astype(BF16)
    for o in range(HALVES):
        u = U_OF[o]
        at96 = iota((96, 384), 0)
        lane96 = iota((96, 384), 1)
        spread = jnp.where(at96 == 32 * u + lax.div(lane96, 8), 1.0, 0.0).astype(BF16)
        len_row = dot(lens_b, spread)[0:1]
        row = iota((256, 384), 0)
        lane = iota((256, 384), 1)
        sample = lax.div(lax.rem(row, 128), 4)
        step = lax.div(row, 128)
        cached = (lane < 256) & (lax.div(lane, 8) == sample) & (
            lax.rem(lane, 8).astype(F32) < jnp.broadcast_to(len_row, (256, 384))
        )
        new_at = lane - 256
        new = (lane >= 256) & (lane < 320) & (lax.rem(new_at, 32) == sample) & (
            lax.div(new_at, 32) <= step
        )
        qu = jnp.concatenate([q[0, o], q[1, o]], axis=0)
        s = jnp.where(cached | new, dot_t(qu, ck[o]), NEG)
        top = jnp.max(s, axis=1, keepdims=True)
        p = jnp.exp2(s * C2 - top * C2)
        own_m[o] = jnp.broadcast_to(top * SCALE, (256, HD))
        own_l[o] = jnp.broadcast_to(jnp.sum(p, axis=1, keepdims=True), (256, HD))
        own_acc[o] = dot(p.astype(BF16), cv[o])

    local(heads_all, heads_all, rs.at[0]).wait()
    inv_v[...] = jnp.sum(tab[...], axis=0)
    to_smem = local(inv_v, inv_s, ld.at[16])
    to_smem.start()
    to_smem.wait()

    def slot_block(s):
        return jnp.clip(inv_s[0, s], 0, BLOCKS - 1)

    def block_slot(n):
        return jnp.clip(inv_s[0, SLOTS + n], 0, SLOTS - 1)

    local(mid, mid, rs.at[1]).wait()

    def select(d):
        for e in range(OWN):
            snd[d, e] = mid[slot_block(OWN * d + e)]

    def to_owner(d):
        return remote(snd.at[d], qin.at[my_t, yy, my_m], ss.at[2], rs.at[2 + my_t], inst=d)

    def send_selected(k, _):
        z = lax.rem(zz + far_first(k, NZ), NZ)
        for y in (1 - yy, yy):
            d = y * NZ + z
            select(d)
            to_owner(d).start()
        return 0

    lax.fori_loop(0, NZ - 1, send_selected, 0)
    select(across)
    to_owner(across).start()
    select(inst)
    local(snd.at[inst], qin.at[my_t, yy, my_m], rs.at[2 + my_t]).start()
    left_of(snd.at[pl.ds(0, NI - 1)], ss.at[2])

    load_k.wait()
    load_v.wait()
    eye = iota((HD, HD), 0) == iota((HD, HD), 1)
    for t in range(2):
        local(qin.at[t], qin.at[t], rs.at[2 + t]).wait()
        for e in range(OWN):
            qv = qin[t, :, :, e].reshape(256, HD)
            top = jnp.full((256, 1), NEG, F32)
            acc = jnp.zeros((256, 2 * HD), F32)
            for c in range(KEYS // KC):
                s = dot_t(qv, kk[e, pl.ds(KC * c, KC)])
                part = s[:, :HD]
                for j in range(1, KC // HD):
                    part = jnp.maximum(part, s[:, HD * j : HD * (j + 1)])
                higher = jnp.maximum(top, jnp.max(part, axis=1, keepdims=True))
                p = jnp.exp2(s * C2 - higher * C2)
                again = jnp.exp2((top - higher) * C2)
                acc = acc * again + dot(p.astype(BF16), va[e, pl.ds(KC * c, KC)])
                top = higher
            weight = acc[:, HD:]
            obuf[t, :, :, e] = (acc[:, :HD] / weight).astype(BF16).reshape(2, 8, 16, HD)
            total = top * SCALE + jnp.log(weight)
            for y in range(2):
                tvec[t, y, e] = jnp.sum(
                    jnp.where(eye, total[HD * y : HD * (y + 1)], 0.0), axis=0, keepdims=True
                )
        base = bases[t]
        slots = mid2.at[pl.ds(OWN * inst, OWN)]
        slots_t = tmid.at[pl.ds(OWN * inst, OWN)]

        def back_to(y, z):
            d = y * NZ + z
            remote(obuf.at[t, y, lax.div(z, 2)], slots, ss.at[4], rs.at[4], inst=d).start()

            @pl.when(lax.rem(z, 8) < 4)
            def _():
                remote(tvec.at[t, y], slots_t, ss.at[5], rs.at[5], inst=d).start()

        def back(k, _):
            z = lax.rem(base + 2 * far_first(k, 8), NZ)
            for y in (1 - yy, yy):
                back_to(y, z)
            return 0

        lax.fori_loop(0, 7, back, 0)
        back_to(1 - yy, base)

        @pl.when(my_t == t)
        def _():
            local(obuf.at[t, yy, my_m], slots, rs.at[4]).start()

            @pl.when(has_totals)
            def _():
                local(tvec.at[t, yy], slots_t, rs.at[5]).start()
                local(tvec.at[t, yy], spare.at[pl.ds(BLOCKS // 4, OWN)], ss.at[5]).start()

        @pl.when(my_t != t)
        def _():
            back_to(yy, base)

    left_of(mid2.at[pl.ds(0, OWN * (NI - 1))], ss.at[4])

    left_of(tmid.at[pl.ds(0, OWN * 16)], ss.at[5])

    local(mid2, mid2, rs.at[4]).wait()

    def home(d):
        n0, n1 = lax.div(HALVES * d, 2), lax.div(HALVES * d + 1, 2)
        outer = (n0, n0 + 1), snd2.at[pl.ds(n0, 2)], pin.at[my_t, my_m, pl.ds(0, 2)]
        inner = (n1,), snd2.at[n1], pin.at[my_t, my_m, 2]
        for (blocks, src, dst), parity in ((outer, 0), (inner, 1)):

            @pl.when(lax.rem(d + yy, 2) == parity)
            def _():
                for n in blocks:
                    snd2[n] = mid2[block_slot(n)]

                @pl.when(d == inst)
                def _():
                    local(src, dst, rs.at[6 + my_t]).start()

                @pl.when(d != inst)
                def _():
                    remote(src, dst, ss.at[6], rs.at[6 + my_t], inst=d).start()

    def home_first(z, _):
        for y in (1 - yy, yy):
            home(y * NZ + z)
        return 0

    lax.fori_loop(0, EARLY, home_first, 0)

    def home_others(k, _):
        z = lax.rem(zz + far_first(k, NZ), NZ)

        @pl.when(z >= EARLY)
        def _():
            for y in (1 - yy, yy):
                home(y * NZ + z)

        return 0

    @pl.when(has_totals)
    def _():
        local(tmid, tmid, rs.at[5]).wait()

        def total_home(i, _):
            n = 2 * lax.div(my_m, 4) + lax.rem(my_m, 2) + 4 * i
            tsnd[i] = tmid[block_slot(n)]
            d = lax.div(2 * n + yy, HALVES)
            to = tin.at[my_t, lax.rem(2 * lax.rem(2 * n + yy, HALVES), HALVES)]

            @pl.when(d == inst)
            def _():
                local(tsnd.at[i], to, rs.at[8 + my_t]).start()
                local(tsnd.at[i], spare.at[i], ss.at[7]).start()

            @pl.when(d != inst)
            def _():
                remote(tsnd.at[i], to, ss.at[7], rs.at[8 + my_t], inst=d).start()

            return 0

        lax.fori_loop(0, BLOCKS // 4, total_home, 0)

    lax.fori_loop(0, NZ, home_others, 0)
    left_halves(snd2, ss.at[6])

    def left_totals():
        @pl.when(has_totals)
        def _():
            local(tsnd, tsnd, ss.at[7]).wait()

    left.append(left_totals)

    load_w.wait()
    for t in range(2):
        local(pin.at[t], pin.at[t], rs.at[6 + t]).wait()
        local(tin.at[t], tin.at[t], rs.at[8 + t]).wait()
        for o in range(HALVES):
            total = jnp.sum(
                jnp.where(eye, jnp.broadcast_to(tin[t, o], (HD, HD)), 0.0), axis=1, keepdims=True
            )
            rows = pl.ds(HD * t, HD)
            own_top = own_m[o, rows]
            top = jnp.maximum(total, own_top)
            carried = jnp.exp(total - top)
            own = jnp.exp(own_top - top)
            below = carried + own * own_l[o, rows]
            before = pin[t, :, o].reshape(HD, HD).astype(F32)
            att[t, pl.ds(HD * U_OF[o], HD)] = (carried * before + own * own_acc[o, rows]) / below
        att[t, pl.ds(384, 16)] = jnp.zeros((16, HD), F32)
        for c in range(2):
            for a in range(0, 8, 2):
                for h in range(4):
                    pair = [att[t, pl.ds(24 * (2 * b + c) + h, 8, stride=4)] for b in (a, a + 1)]
                    lhs[t, pl.ds(64 * c + 8 * a, 16), pl.ds(HD * h, HD)] = jnp.concatenate(
                        pair, axis=0
                    ).astype(BF16)
        for c in range(NCH):
            part = dot(lhs[t], w[:, pl.ds(CH * c, CH)])
            cs[t, c] = jnp.where(core == 0, part[64:], part[:64]).astype(BF16)
            mine[t, c] = jnp.where(core == 0, part[:64], part[64:])
            remote(
                cs.at[t, c], cr.at[t, c], css.at[2 * t + c], crs.at[2 * t + c], tp=partner
            ).start()
        for c in range(NCH):
            pair_copy = remote(
                cs.at[t, c], cr.at[t, c], css.at[2 * t + c], crs.at[2 * t + c], tp=partner
            )
            pair_copy.wait_recv()
            left.append(pair_copy.wait_send)
            both = (mine[t, c] + cr[t, c].astype(F32)).reshape(8, 8, CH)
            rest = both[:, :, 2 * PK :]
            rest = jnp.concatenate([rest[:, :4], rest[:, 4:8]], axis=2)
            both = jnp.concatenate([both[:, :6, :PK], both[:, :6, PK : 2 * PK], rest], axis=1)
            sums[t, c] = both
            xs[t, c] = both.astype(BF16)

            for n, (dx, dy) in enumerate(CHIPS):
                to = lax.rem(lax.div(chip, 2) + dx, 4) * 2 + lax.rem(chip + dy, 2)
                remote(
                    xs.at[t, c, to],
                    xr.at[t, c, n],
                    xss.at[2 * t + c],
                    xrs.at[2 * t + c],
                    tp=2 * to + core,
                ).start()
            left_of(xr.at[t, c], xss.at[2 * t + c])
    for wait in left:
        wait()
    for t in range(2):
        for c in range(NCH):
            local(xr.at[t, c], xr.at[t, c], xrs.at[2 * t + c]).wait()
            total = sums[t, c, chip]
            for n in range(7):
                total = total + xr[t, c, n].astype(F32)
            if t == 0:
                step0[c] = total
                continue
            for r in range(6):
                last = (12 + r, 0) if r < 4 else (8 + r, PK // 2)
                for at, lane, to, width in (
                    (r, 0, 0, PK),
                    (6 + r, 0, PK, PK),
                    (*last, 2 * PK, PK // 2),
                ):
                    out[r, :, pl.ds(CH * c + to, width)] = jnp.concatenate(
                        [
                            step0[c, pl.ds(at, 1), pl.ds(lane, width)],
                            total[at : at + 1, lane : lane + width],
                        ],
                        axis=0,
                    ).astype(BF16)


def shards(
    queries,
    row_prompt,
    owner_slot,
    suffix_len,
    prefix_keys,
    prefix_values,
    suffix_keys,
    suffix_values,
    new_keys,
    new_values,
    out_weight,
):
    vmem = pl.BlockSpec(memory_space=pltpu.VMEM)
    hbm = pl.BlockSpec(memory_space=pl.ANY)
    sem = pltpu.SemaphoreType.DMA
    scratch = [
        pltpu.SMEM((96,), I32),
        pltpu.SMEM((48,), I32),
        pltpu.VMEM((1, 96), I32),
        pltpu.VMEM((2, HALVES, 128, HD), BF16),
        pltpu.VMEM((OWN, KEYS, HD), BF16),
        pltpu.VMEM((OWN, KEYS, 2 * HD), BF16),
        pltpu.VMEM((HALVES, 384, HD), BF16),
        pltpu.VMEM((HALVES, 384, HD), BF16),
        pltpu.VMEM((512, D), BF16),
        pltpu.VMEM((NI, 1, HD), I32),
        pltpu.VMEM((1, HD), I32),
        pltpu.SMEM((1, HD), I32),
        pltpu.VMEM((BLOCKS, 16, HD), BF16),
        pltpu.VMEM((NI, OWN, 16, HD), BF16),
        pltpu.VMEM((2, 2, 8, OWN, 16, HD), BF16),
        pltpu.VMEM((2, 2, 8, OWN, 16, HD), BF16),
        pltpu.VMEM((SLOTS, 16, HD), BF16),
        pltpu.VMEM((BLOCKS, 16, HD), BF16),
        pltpu.VMEM((2, 8, HALVES, 16, HD), BF16),
        pltpu.VMEM((2, 2, OWN, 1, HD), F32),
        pltpu.VMEM((SLOTS, 1, HD), F32),
        pltpu.VMEM((BLOCKS // 4, 1, HD), F32),
        pltpu.VMEM((BLOCKS // 4 + OWN, 1, HD), F32),
        pltpu.VMEM((2, HALVES, 1, HD), F32),
        pltpu.VMEM((HALVES, 256, HD), F32),
        pltpu.VMEM((HALVES, 256, HD), F32),
        pltpu.VMEM((HALVES, 256, HD), F32),
        pltpu.VMEM((2, 400, HD), F32),
        pltpu.VMEM((2, 128, 512), BF16),
        pltpu.VMEM((2, NCH, 64, CH), F32),
        pltpu.VMEM((2, NCH, 64, CH), BF16),
        pltpu.VMEM((2, NCH, 64, CH), BF16),
        pltpu.VMEM((2, NCH, 8, 16, PK), BF16),
        pltpu.VMEM((2, NCH, 7, 16, PK), BF16),
        pltpu.VMEM((2, NCH, 8, 16, PK), F32),
        pltpu.VMEM((NCH, 16, PK), F32),
        sem((20,)),
        sem((8,)),
        sem((10,)),
        sem((2 * NCH,)),
        sem((2 * NCH,)),
        sem((2 * NCH,)),
        sem((2 * NCH,)),
    ]
    return pl.pallas_call(
        kernel,
        out_shape=jax.ShapeDtypeStruct((6, 2, D), BF16),
        in_specs=[hbm] * 11,
        out_specs=vmem,
        scratch_shapes=scratch,
        compiler_params=pltpu.CompilerParams(
            collective_id=0, has_side_effects=True, vmem_limit_bytes=56 * 1024 * 1024
        ),
    )(
        row_prompt,
        owner_slot,
        suffix_len.reshape(1, 96),
        queries.reshape(2, 384, HD),
        prefix_keys.reshape(OWN, KEYS, HD),
        prefix_values.reshape(OWN, KEYS, HD),
        suffix_keys.reshape(768, HD),
        suffix_values.reshape(768, HD),
        new_keys.reshape(2, 96, HD),
        new_values.reshape(2, 96, HD),
        out_weight,
    )


def solution(mesh):
    placed = (
        P(None, "inst", "tp", None),
        P("inst"),
        P(),
        P("inst"),
        P("inst", None, "tp", None),
        P("inst", None, "tp", None),
        P("inst", None, "tp", None),
        P("inst", None, "tp", None),
        P(None, "inst", "tp", None),
        P(None, "inst", "tp", None),
        P("tp", None),
    )
    return jax.shard_map(
        shards, mesh=mesh, in_specs=placed, out_specs=P(("inst", "tp"), None, None), check_vma=False
    )
```
